512 devices in a mesh: dp: 128 (over x, z, core), mp: 4 (over y).
Axes of the slice: x: 4, y: 4, z: 16, core: 2. Of those that a mesh axis runs over, the one named last changes fastest.
Arguments:
- q_hidden: bfloat16 [8192, 4096], P('dp', 'mp'), may hold values from -0.09375 to 0.09375
- p_hidden: bfloat16 [8192, 4096], P('dp', 'mp'), may hold values from -0.09375 to 0.09375
- proj: bfloat16 [4096, 4096], P('dp', 'mp'), may hold values from -0.25 to 0.25
- positives: int32 [8192], P('dp'), may hold values from 0 to 8191, as said below
- negatives: int32 [8192, 16], P('dp'), may hold values from 0 to 8191, as said below
Outputs:
- grad_q_hidden: bfloat16 [8192, 4096], P('dp', 'mp')
- grad_p_hidden: bfloat16 [8192, 4096], P('dp', 'mp')
- query_loss: float32 [8192], P('dp')
The draws below stay inside these ranges and needn't reach their ends.
Inputs may be any that keep to these rules, and one draw needn't show every extreme that they name: `positives`: the positive of a query is a passage held by the same index of dp as the query (passages i * 64 to (i + 1) * 64 - 1 on index i), and each such passage is the positive of exactly one of that device's queries. Passage p is held by index p // 64 of dp. The 1024 negatives of one index's queries name, counting repeats, at most 12 passages held by any one index; one index is named exactly 12 times by the queries of every index. Negatives are mined per device from a shared pool: for each holder, a device's queries draw from the same four passages of that holder. A query's negatives are four runs of four consecutive entries; each run names those four distinct passages of one holder, and all runs that one index's queries direct to one holder name them in the same order. A negative may repeat or equal the positive.
All inputs are finite; a program needn't handle non-finite values.
Results may differ from the reference program's by a relative error of at most 0.019.
Values may be sent and summed in bfloat16 or wider, within the bound.
A program may use at most 128 MiB of HBM per device.

```python
import math
import jax
import jax.numpy as jnp
from jax import lax

D = 4096
Q_DEV = 64
NEG = 16
QUERIES = 8192
PASSAGES = 8192
N_MP = 4


HIDDEN_STD = 0.015625


HIDDEN_BOUND = 0.09375


SHARED = 0.08


def positive_ids(key):
    key = jax.random.fold_in(key, 5)
    device_count = QUERIES // Q_DEV
    keys = jax.random.split(key, device_count)

    def shuffle_rows(dev_key):
        return jax.random.permutation(dev_key, Q_DEV).astype(jnp.int32)
    shuffled = jax.vmap(shuffle_rows)(keys)
    base_ids = (jnp.arange(device_count, dtype=jnp.int32) * Q_DEV)[:, None]
    return (shuffled + base_ids).reshape(-1).astype(jnp.int32)


def noise_pair(key, salt):
    noise_key = jax.random.fold_in(key, salt)
    normal_part = jax.random.normal(noise_key, (QUERIES, D), jnp.float32)
    return normal_part


def draw_positives(key, part):
    return positive_ids(key)


def draw_q_hidden(key, part):
    normal_part = noise_pair(key, 11)
    base = normal_part
    return jnp.clip(base * HIDDEN_STD, -HIDDEN_BOUND, HIDDEN_BOUND).astype(jnp.bfloat16)


def draw_p_hidden(key, part):
    query_normal = noise_pair(key, 11)
    own_normal = noise_pair(key, 13)
    query_base = query_normal
    own_base = own_normal
    pos_ids = positive_ids(key)
    moved = jnp.zeros((PASSAGES, D), jnp.float32).at[pos_ids].set(query_base)
    mixed = math.sqrt(SHARED) * moved + math.sqrt(1.0 - SHARED) * own_base
    return jnp.clip(mixed * HIDDEN_STD, -HIDDEN_BOUND, HIDDEN_BOUND).astype(jnp.bfloat16)


def draw_proj(key, part):
    key = jax.random.fold_in(key, 17)
    entry_key, column_key = jax.random.split(key)
    entries = jax.random.normal(entry_key, (D, D), jnp.float32)
    position = jnp.arange(D, dtype=jnp.float32) / D
    rough = jnp.exp(jax.random.uniform(column_key, (D,), jnp.float32, -0.35, 0.35))
    column_gain = (1.0 + 3.0 * position) / math.sqrt(7.0)
    scaled = entries * (column_gain * rough)[None, :] / math.sqrt(D)
    return jnp.clip(scaled, -0.25, 0.25).astype(jnp.bfloat16)


def draw_negatives(key, part):
    key = jax.random.fold_in(key, 9)
    device_count = QUERIES // Q_DEV
    slot_count = NEG * Q_DEV
    mean_load = slot_count // device_count
    half_load = mean_load // 2
    hot_key, rest_key = jax.random.split(key)
    hot_owner = jax.random.randint(hot_key, (), 0, device_count)
    rank_pos = jnp.arange(device_count, dtype=jnp.int32)
    rank_load = jnp.where(rank_pos < device_count // 4, mean_load + half_load, jnp.where(rank_pos < device_count // 2, mean_load - half_load, mean_load)).astype(jnp.int32)

    def one_device(dev_key):
        key_order, key_groups, key_pick = jax.random.split(dev_key, 3)
        order_score = jax.random.permutation(key_order, device_count).astype(jnp.int32)
        order_score = jnp.where(rank_pos == hot_owner, -1, order_score)
        order = jnp.argsort(order_score)
        owner_load = jnp.zeros((device_count,), jnp.int32).at[order].set(rank_load)
        bounds = jnp.cumsum(owner_load)
        starts = bounds - owner_load
        slot_pos = jnp.arange(slot_count, dtype=jnp.int32)
        owners = jnp.searchsorted(bounds, slot_pos, side='right').astype(jnp.int32)
        within = slot_pos - starts[owners]
        pick_keys = jax.random.split(key_pick, device_count)

        def pick_four(pick_key):
            return jax.random.permutation(pick_key, Q_DEV)[:4].astype(jnp.int32)
        picks = jax.vmap(pick_four)(pick_keys)
        local_ids = picks[owners, within % 4]
        ids = owners * Q_DEV + local_ids
        group_order = jax.random.permutation(key_groups, slot_count // 4)
        return ids.reshape(slot_count // 4, 4)[group_order].reshape(Q_DEV, NEG)
    keys = jax.random.split(rest_key, device_count)
    return jax.vmap(one_device)(keys).reshape(QUERIES, NEG).astype(jnp.int32)


def setup_inputs(seed: int = 0) -> dict:
    splits = jax.random.split(jax.random.key(seed), 6)
    return {
        "q_hidden": draw_q_hidden(jax.random.fold_in(splits[5], 71), 0),
        "p_hidden": draw_p_hidden(jax.random.fold_in(splits[5], 71), 0),
        "proj": draw_proj(jax.random.fold_in(splits[5], 71), 0),
        "positives": draw_positives(jax.random.fold_in(splits[5], 71), 0),
        "negatives": draw_negatives(jax.random.fold_in(splits[5], 71), 0),
    }


SCALE = 20.0
EPS = 1e-06

def embed_rows(hidden, proj):
    rounded = jnp.dot(hidden, proj, preferred_element_type=jnp.float32).astype(jnp.bfloat16)
    widened = lax.optimization_barrier(rounded).astype(jnp.float32)
    radius = jnp.sqrt(lax.optimization_barrier(jnp.sum(widened * widened, axis=1)) + EPS)
    unit_exact = widened / radius[:, None]
    return (unit_exact, radius, unit_exact.astype(jnp.bfloat16))

def unit_backward(grad_unit, unit_exact, radius):
    inner = lax.optimization_barrier(jnp.sum(unit_exact * grad_unit, axis=1))
    return ((grad_unit - unit_exact * inner[:, None]) / radius[:, None]).astype(jnp.bfloat16)

def project_back(grad_emb, proj):
    block_width = D // N_MP
    summed = jnp.zeros((grad_emb.shape[0], D), jnp.float32)
    for block_index in range(N_MP):
        low = block_index * block_width
        partial_term = jnp.dot(grad_emb[:, low:low + block_width], proj[:, low:low + block_width].T, preferred_element_type=jnp.float32)
        partial_term = lax.optimization_barrier(partial_term.astype(jnp.bfloat16))
        summed = summed + partial_term.astype(jnp.float32)
    return summed.astype(jnp.bfloat16)

def reference(q_hidden, p_hidden, proj, positives, negatives):
    q_exact, q_radius, q_unit = embed_rows(q_hidden, proj)
    p_exact, p_radius, p_unit = embed_rows(p_hidden, proj)
    cand = jnp.concatenate([positives[:, None], negatives], axis=1).astype(jnp.int32)
    block_size = math.gcd(QUERIES, 512)
    block_count = QUERIES // block_size
    width_cand = NEG + 1
    target = (jnp.arange(width_cand) == 0).astype(jnp.float32)

    def one_block(grad_pass, block_in):
        query_block, cand_block = block_in
        rows_cand = p_unit[cand_block.reshape(-1)].reshape(block_size, width_cand, D)
        cand_wide = rows_cand.astype(jnp.float32)
        query_wide = query_block.astype(jnp.float32)
        scores = SCALE * jnp.einsum('qd,qkd->qk', query_wide, cand_wide, precision=lax.Precision.HIGHEST)
        exp_scores = jnp.exp(scores)
        denominator = lax.optimization_barrier(jnp.sum(exp_scores, axis=1))
        probs = exp_scores / denominator[:, None]
        block_loss = jnp.log(denominator) - scores[:, 0]
        coef = SCALE * (probs - target[None, :])
        grad_query = jnp.einsum('qk,qkd->qd', coef, cand_wide, precision=lax.Precision.HIGHEST)
        terms = (coef[:, :, None] * query_wide[:, None, :]).astype(jnp.bfloat16)
        grad_pass = grad_pass.at[cand_block.reshape(-1)].add(terms.reshape(-1, D).astype(jnp.float32))
        return (grad_pass, (block_loss, grad_query))
    start_grad = jnp.zeros((PASSAGES, D), jnp.float32)
    inputs_scan = (q_unit.reshape(block_count, block_size, D), cand.reshape(block_count, block_size, width_cand))
    g_punit, outputs_scan = lax.scan(one_block, start_grad, inputs_scan)
    query_loss = outputs_scan[0].reshape(QUERIES)
    g_qunit = outputs_scan[1].reshape(QUERIES, D)
    g_qemb = unit_backward(g_qunit, q_exact, q_radius)
    g_pemb = unit_backward(g_punit, p_exact, p_radius)
    return (project_back(g_qemb, proj), project_back(g_pemb, proj), query_loss)
```

```python
import functools

import jax
import jax.numpy as jnp
from jax import lax
from jax.experimental import pallas as pl
from jax.experimental.pallas import tpu as pltpu
from jax.sharding import PartitionSpec as P

SCALE = 20.0
EPS = 1e-06
MESH = pl.DeviceIdType.MESH
F32 = jnp.float32
BF16 = jnp.bfloat16

NX, NZ, NC, NY = 4, 16, 2, 4
NDP = NX * NZ * NC
NPEER = NX * NC
HALF = NZ // 2
RUN = 4
CAP = 3
KINDS = 8


def coords():
    dp = lax.axis_index("dp")
    y = lax.axis_index("mp")
    core = lax.rem(dp, NC)
    chip = lax.div(dp, NC)
    return lax.div(chip, NZ), y, lax.rem(chip, NZ), core


def dp_index(x, z, core):
    return (x * NZ + z) * NC + core


def wrap(value, size):
    return lax.rem(value + 2 * size, size)


def remote(src, dst, send_sem, recv_sem, dp, y):
    return pltpu.make_async_remote_copy(
        src_ref=src,
        dst_ref=dst,
        send_sem=send_sem,
        recv_sem=recv_sem,
        device_id=(dp, y),
        device_id_type=MESH,
    )


def greet(peers):
    barrier = pltpu.get_barrier_semaphore()
    for dp, y in peers:
        pl.semaphore_signal(barrier, inc=1, device_id=(dp, y), device_id_type=MESH)
    pl.semaphore_wait(barrier, len(peers))


def embed_kernel(
    hq_ref, hp_ref, w_ref, emb_ref, wout_ref, hid, wbuf, y_s, y_r, x_s, x_r, z_s, z_r, c_s, c_r, o_s
):
    x, y, z, core = coords()
    me = dp_index(x, z, core)
    rows_q = hq_ref.shape[0]
    depth = w_ref.shape[0]
    width = w_ref.shape[1]
    half_w = width // 2
    right = dp_index(x, wrap(z + 1, NZ), core)
    left = dp_index(x, wrap(z - 1, NZ), core)
    sibling = dp_index(x, z, 1 - core)
    y_peers = [wrap(y + k, NY) for k in range(1, NY)]
    x_peers = [dp_index(wrap(x + k, NX), z, core) for k in range(1, NX)]
    greet(
        [(me, p) for p in y_peers] + [(p, y) for p in x_peers] + [(right, y), (left, y), (sibling, y)]
    )

    def rows_of(zb):
        return pl.ds(pl.multiple_of((zb * NC + core) * depth, depth), depth)

    def w_slice(zb, piece):
        return wbuf.at[:, rows_of(zb), pl.ds(piece * half_w, half_w)]

    wbuf[x, rows_of(z), :] = w_ref[...]
    pending = []
    x_copies = []
    for k, peer in enumerate(x_peers):
        own = wbuf.at[x, rows_of(z)]
        cp = remote(own, own, x_s.at[k], x_r.at[k], peer, y)
        cp.start()
        x_copies.append(cp)
    hid[y, 0:rows_q, :] = hq_ref[...]
    hid[y, rows_q : 2 * rows_q, :] = hp_ref[...]
    y_copies = []
    for k, peer in enumerate(y_peers):
        cp = remote(hid.at[y], hid.at[y], y_s.at[k], y_r.at[k], me, peer)
        cp.start()
        y_copies.append(cp)
    for cp in x_copies:
        cp.wait()

    def to_sibling(zb, piece, slot):
        cp = remote(
            w_slice(zb, piece), w_slice(zb, piece), c_s.at[slot, piece], c_r.at[slot, piece], sibling, y
        )
        cp.start()
        pending.append(cp)

    def ring(direction, step, piece):
        zb = wrap(z - (step - 1), NZ) if direction == 0 else wrap(z + (step - 1), NZ)
        return remote(
            w_slice(zb, piece),
            w_slice(zb, piece),
            z_s.at[direction, step - 1, piece],
            z_r.at[direction, step - 1, piece],
            right if direction == 0 else left,
            y,
        )

    live = {}
    for piece in range(2):
        for direction in range(2):
            cp = ring(direction, 1, piece)
            cp.start()
            live[direction, 1, piece] = cp
    for piece in range(2):
        to_sibling(z, piece, 0)
    for step in range(1, HALF + 1):
        for piece in range(2):
            for direction in range(2):
                if (direction, step, piece) not in live:
                    continue
                live[direction, step, piece].wait_recv()
                last = step + 1 == HALF
                if step + 1 < HALF or (last and direction == piece):
                    cp = ring(direction, step + 1, piece)
                    cp.start()
                    live[direction, step + 1, piece] = cp
                zb = wrap(z - step, NZ) if direction == 0 else wrap(z + step, NZ)
                to_sibling(zb, piece, step if direction == 0 or step == HALF else HALF + step)
    for cp in live.values():
        cp.wait_send()
    for cp in pending:
        cp.wait()
    for cp in y_copies:
        cp.wait()
    out = pltpu.make_async_copy(wbuf, wout_ref, o_s)
    out.start()
    tile = 256

    @pl.loop(0, width // tile)
    def _(t):
        cols = pl.ds(pl.multiple_of(t * tile, tile), tile)
        total = jnp.zeros((2 * rows_q, tile), F32)
        for b in range(NY):
            total = total + jnp.dot(hid[b], wbuf[b, :, cols], preferred_element_type=F32)
        emb_ref[:, cols] = total.astype(BF16)

    out.wait()


def embed(q_hidden, p_hidden, proj):
    rows = q_hidden.shape[0]
    width = q_hidden.shape[1]
    depth = proj.shape[0]
    block = depth * NDP // NX
    vmem = pl.BlockSpec(memory_space=pltpu.VMEM)
    dma = pltpu.SemaphoreType.DMA
    return pl.pallas_call(
        embed_kernel,
        out_shape=(
            jax.ShapeDtypeStruct((2 * rows, width), BF16),
            jax.ShapeDtypeStruct((NX, block, width), BF16),
        ),
        in_specs=[vmem] * 3,
        out_specs=(vmem, pl.BlockSpec(memory_space=pl.ANY)),
        scratch_shapes=[
            pltpu.VMEM((NY, 2 * rows, width), BF16),
            pltpu.VMEM((NX, block, width), BF16),
            dma((NY - 1,)),
            dma((NY - 1,)),
            dma((NX - 1,)),
            dma((NX - 1,)),
            dma((2, HALF, 2)),
            dma((2, HALF, 2)),
            dma((NZ, 2)),
            dma((NZ, 2)),
            dma,
        ],
        compiler_params=pltpu.CompilerParams(
            collective_id=0, has_side_effects=True, vmem_limit_bytes=48 * 1024 * 1024
        ),
        cost_estimate=pl.CostEstimate(
            flops=2 * 2 * rows * width * NY * width, bytes_accessed=100 * 1024 * 1024, transcendentals=0
        ),
        name="gather_embed",
    )(q_hidden, p_hidden, proj)


def nt(a, b):
    return lax.dot_general(a, b, (((1,), (1,)), ((), ())), preferred_element_type=F32)


def loss_kernel(
    emb_ref,
    w_hbm,
    sel_ref,
    idx_ref,
    part_ref,
    gq_ref,
    gp_ref,
    loss_ref,
    wbuf,
    col,
    outbox,
    recv,
    ybuf,
    dz,
    dtab,
    gpart,
    gin,
    acc,
    w_s,
    z_s,
    z_r,
    p_s,
    p_r,
    y_s,
    y_r,
    d_s,
    d_r,
    e_s,
    e_r,
    g_s,
    g_r,
):
    x, y, z, core = coords()
    me = dp_index(x, z, core)
    rank = x * NC + core
    rows2 = emb_ref.shape[0]
    rows = rows2 // 2
    width = emb_ref.shape[1]
    half_w = width // 2
    right = dp_index(x, wrap(z + 1, NZ), core)
    left = dp_index(x, wrap(z - 1, NZ), core)

    def peer_of(k):
        other = wrap(rank + k, NPEER)
        return dp_index(lax.div(other, NC), z, lax.rem(other, NC))

    y_peers = [wrap(y + k, NY) for k in range(1, NY)]
    z_peers = [dp_index(x, wrap(z + k, NZ), core) for k in range(1, NZ)]
    mates = [peer_of(k) for k in range(1, NPEER)]
    greet([(me, p) for p in y_peers] + [(p, y) for p in z_peers] + [(p, y) for p in mates])

    w_copy = pltpu.make_async_copy(w_hbm, wbuf, w_s)
    w_copy.start()
    col[0, 0:rows2, :] = emb_ref[...]

    def ring(direction, step, piece):
        src_at = piece * rows if direction == 0 or step == 1 else rows2 + piece * rows
        if step < HALF:
            src = col.at[step - 1, pl.ds(src_at, rows)]
            dst = col.at[step, pl.ds(direction * rows2 + piece * rows, rows)]
        else:
            cols = pl.ds(direction * half_w, half_w)
            src = col.at[step - 1, pl.ds(src_at, rows), cols]
            dst = col.at[0, pl.ds(rows2 + piece * rows, rows), cols]
        return remote(
            src,
            dst,
            z_s.at[direction, step - 1, piece],
            z_r.at[direction, step - 1, piece],
            right if direction == 0 else left,
            y,
        )

    live = {}
    sends = []
    for piece in range(2):
        for direction in range(2):
            live[direction, 1, piece] = ring(direction, 1, piece)
            live[direction, 1, piece].start()

    pair_rows = lax.broadcasted_iota(jnp.int32, (2 * rows2, NPEER * 2 * KINDS), 0)
    for step in range(1, HALF + 1):
        for piece in range(2):
            for direction in range(2):
                live[direction, step, piece].wait_recv()
                if step < HALF:
                    cp = ring(direction, step + 1, piece)
                    cp.start()
                    live[direction, step + 1, piece] = cp
        slot = step % HALF
        pick = (pair_rows == sel_ref[slot : slot + 1, :]).astype(F32).astype(BF16)
        rows_out = lax.dot_general(
            pick, col[slot], (((0,), (0,)), ((), ())), preferred_element_type=F32
        )
        outbox[slot] = rows_out.astype(BF16).reshape(NPEER, 2 * KINDS, width)
        for k, peer in enumerate(mates):
            cp = remote(
                outbox.at[slot, wrap(rank + k + 1, NPEER)],
                recv.at[rank, slot],
                p_s.at[slot, k],
                p_r.at[slot, k],
                peer,
                y,
            )
            cp.start()
            sends.append(cp)
        recv[rank, slot] = outbox[slot, rank]
    for cp in live.values():
        cp.wait_send()

    lane = lax.broadcasted_iota(jnp.int32, (1, rows2), 1)
    row_id = lax.broadcasted_iota(jnp.int32, (rows2, rows2), 0)
    eye = row_id == lax.broadcasted_iota(jnp.int32, (rows2, rows2), 1)
    emb = col[0, 0:rows2, :]
    pair = row_id == part_ref[0:1, :]

    def down(mask, value):
        return jnp.sum(jnp.where(mask, value, 0.0), axis=0, keepdims=True)

    def across(mask, value):
        return jnp.sum(jnp.where(mask, value, 0.0), axis=1, keepdims=True)

    def mask_of(d, r):
        return row_id == idx_ref[d, r : r + 1, :]

    gram = nt(emb, emb)
    own_sq = down(eye, gram)
    own_pos = down(pair, gram)
    for cp in sends:
        cp.wait()
    for d in range(NPEER):
        got = recv[d].reshape(rows2, width)
        cross = nt(emb, got)
        parts = [down(mask_of(d, r), cross) for r in range(RUN)]
        parts += [down(eye, nt(got, got)), own_sq, own_pos, jnp.zeros_like(own_sq)]
        ybuf[y, d] = jnp.concatenate(parts, axis=0)
    y_copies = []
    for k, peer in enumerate(y_peers):
        cp = remote(ybuf.at[y], ybuf.at[y], y_s.at[k], y_r.at[k], me, peer)
        cp.start()
        y_copies.append(cp)
    for cp in y_copies:
        cp.wait()

    sums = [((ybuf[0, d] + ybuf[1, d]) + ybuf[2, d]) + ybuf[3, d] for d in range(NPEER)]
    inv_row = 1.0 / jnp.sqrt(sums[0][5:6] + EPS)
    inv_col = across(eye, inv_row)
    pos_score = SCALE * sums[0][6:7] * inv_row * down(pair, inv_col)
    pos_exp = jnp.exp(pos_score)
    denom = across(eye, pos_exp)
    scores = []
    exps = []
    lane_inv = []
    for d in range(NPEER):
        rl = 1.0 / jnp.sqrt(sums[d][4:5] + EPS)
        lane_inv.append(rl)
        sc = []
        ex = []
        for r in range(RUN):
            mask = mask_of(d, r)
            s = SCALE * sums[d][r : r + 1] * rl * down(mask, inv_col)
            e = jnp.exp(s)
            sc.append(s)
            ex.append(e)
            denom = denom + across(mask, e)
        scores.append(sc)
        exps.append(ex)
    denom_row = down(eye, denom)
    loss_ref[...] = jnp.log(denom_row) - pos_score
    is_query = lane < rows
    dinv_row = jnp.where(is_query, 1.0 / denom_row, 0.0)
    dinv_col = across(eye, dinv_row)

    dz[0] = dinv_row
    d_copies = []
    for k, peer in enumerate(z_peers):
        cp = remote(dz.at[0], dz.at[k + 1], d_s.at[k], d_r.at[k], peer, y)
        cp.start()
        d_copies.append(cp)
    for cp in d_copies:
        cp.wait()
    e_copies = []
    for k, peer in enumerate(mates):
        cp = remote(dz, dtab.at[k + 1], e_s.at[k], e_r.at[k], peer, y)
        cp.start()
        e_copies.append(cp)
    for k in range(NZ):
        dtab[0, k] = dz[k]
    for cp in e_copies:
        cp.wait()

    place = lax.broadcasted_iota(jnp.int32, (NZ, rows2), 0)
    lane16 = lax.broadcasted_iota(jnp.int32, (NZ, rows2), 1)
    step16 = lane16 // (2 * KINDS)
    second = (lane16 // KINDS) % 2
    source = jnp.where(
        second == 0, step16, jnp.where(step16 == 0, HALF, NZ - step16)
    )
    at_source = place == source
    inner = jnp.zeros((rows2, 1), F32)
    acc[...] = jnp.zeros_like(acc)

    def add_rows(weights, values):
        high = weights.astype(BF16)
        low = (weights - high.astype(F32)).astype(BF16)
        acc[...] += jnp.dot(high, values, preferred_element_type=F32) + jnp.dot(
            low, values, preferred_element_type=F32
        )

    for d in range(NPEER):
        table = jnp.concatenate([dtab[wrap(rank - d, NPEER), k] for k in range(NZ)], axis=0)
        spread = jnp.where(row_id == idx_ref[d, 4:5, :], 1.0, 0.0)
        found = jnp.dot(table, spread, preferred_element_type=F32, precision=lax.Precision.HIGHEST)
        dl = down(at_source, found)
        weights = jnp.zeros((rows2, rows2), F32)
        for r in range(RUN):
            mask = mask_of(d, r)
            coef = SCALE * exps[d][r] * (down(mask, dinv_col) + dl)
            weights = weights + jnp.where(mask, coef * lane_inv[d], 0.0)
            inner = inner + across(mask, coef * scores[d][r] * (1.0 / SCALE))
        add_rows(weights, recv[d].reshape(rows2, width))
    pos_coef = jnp.where(is_query, SCALE * (pos_exp * dinv_row - 1.0), 0.0)
    pos_coef = pos_coef + down(pair, across(eye, pos_coef))
    add_rows(jnp.where(pair, pos_coef * inv_row, 0.0), emb)
    inner = inner + across(pair, pos_coef * pos_score * (1.0 / SCALE))
    unit = emb.astype(F32) * inv_col
    g_emb = ((acc[...] - unit * inner) * inv_col).astype(BF16)

    w_copy.wait()
    g_copies = []
    for k in range(1, NY + 1):
        block = wrap(y + k, NY)
        gpart[k - 1] = nt(g_emb, wbuf[block]).astype(BF16)
        if k < NY:
            cp = remote(gpart.at[k - 1], gin.at[k - 1], g_s.at[k - 1], g_r.at[k - 1], me, block)
            cp.start()
            g_copies.append(cp)
    total = gpart[NY - 1].astype(F32)
    for k, cp in enumerate(g_copies):
        cp.wait()
        total = total + gin[k].astype(F32)
    grads = total.astype(BF16)
    gq_ref[...] = grads[0:rows]
    gp_ref[...] = grads[rows:]


def loss_grads(emb, w_full, sel, idx, partner):
    rows2, width = emb.shape
    rows = rows2 // 2
    vmem = pl.BlockSpec(memory_space=pltpu.VMEM)
    hbm = pl.BlockSpec(memory_space=pl.ANY)
    dma = pltpu.SemaphoreType.DMA
    return pl.pallas_call(
        loss_kernel,
        out_shape=(
            jax.ShapeDtypeStruct((rows, width), BF16),
            jax.ShapeDtypeStruct((rows, width), BF16),
            jax.ShapeDtypeStruct((1, rows2), F32),
        ),
        in_specs=[vmem, hbm, vmem, vmem, vmem],
        out_specs=(vmem,) * 3,
        scratch_shapes=[
            pltpu.VMEM(w_full.shape, BF16),
            pltpu.VMEM((HALF, 2 * rows2, width), BF16),
            pltpu.VMEM((HALF, NPEER, 2 * KINDS, width), BF16),
            pltpu.VMEM((NPEER, HALF, 2 * KINDS, width), BF16),
            pltpu.VMEM((NY, NPEER, 8, rows2), F32),
            pltpu.VMEM((NZ, 1, rows2), F32),
            pltpu.VMEM((NPEER, NZ, 1, rows2), F32),
            pltpu.VMEM((NY, rows2, width), BF16),
            pltpu.VMEM((NY - 1, rows2, width), BF16),
            pltpu.VMEM((rows2, width), F32),
            dma,
            dma((2, HALF, 2)),
            dma((2, HALF, 2)),
            dma((HALF, NPEER - 1)),
            dma((HALF, NPEER - 1)),
            dma((NY - 1,)),
            dma((NY - 1,)),
            dma((NZ - 1,)),
            dma((NZ - 1,)),
            dma((NPEER - 1,)),
            dma((NPEER - 1,)),
            dma((NY - 1,)),
            dma((NY - 1,)),
        ],
        compiler_params=pltpu.CompilerParams(
            collective_id=1, has_side_effects=True, vmem_limit_bytes=48 * 1024 * 1024
        ),
        cost_estimate=pl.CostEstimate(
            flops=10**9, bytes_accessed=100 * 1024 * 1024, transcendentals=0
        ),
        name="loss_grads",
    )(emb, w_full, sel, idx, partner)


def run_tables(negatives, rows):
    runs = negatives.reshape(-1, RUN)
    count = runs.shape[0]
    owner = runs[:, 0] // rows
    local = runs % rows
    hit = owner[:, None] == jnp.arange(NDP, dtype=jnp.int32)[None, :]
    order = jnp.arange(count, dtype=jnp.int32)
    earlier = (order[:, None] > order[None, :]).astype(BF16)
    rank = jnp.dot(earlier, hit.astype(BF16), preferred_element_type=F32).astype(jnp.int32)
    query = order // (count // rows)
    picked = [
        jnp.max(jnp.where(hit, local[:, j][:, None], 0), axis=0) for j in range(RUN)
    ] + [
        jnp.max(jnp.where(hit & (rank == i), query[:, None], -1), axis=0) for i in range(CAP)
    ]
    return jnp.stack(picked, axis=0)


def body(q_hidden, p_hidden, proj, positives, negatives):
    rows = q_hidden.shape[0]
    x, y, z, core = coords()
    me = lax.axis_index("dp")
    mine = run_tables(negatives, rows)
    tables = lax.all_gather(mine, "dp", axis=0)
    emb, w_full = embed(q_hidden, p_hidden, proj)

    steps = jnp.arange(HALF, dtype=jnp.int32)
    near = jnp.stack(
        [(z - steps + NZ) % NZ, jnp.where(steps == 0, (z + HALF) % NZ, (z + steps) % NZ)], axis=1
    ).reshape(-1)
    order_z = (near[:, None] == jnp.arange(NZ, dtype=jnp.int32)[None, :]).astype(F32)

    def by_step(values):
        return jnp.round(
            jnp.einsum("...z,sz->...s", values.astype(F32), order_z, precision=lax.Precision.HIGHEST)
        ).astype(jnp.int32)

    full = tables.reshape(NX, NZ, NC, RUN + CAP, NX, NZ, NC)
    askers = lax.dynamic_index_in_dim(full, z, 1, keepdims=False)
    askers = lax.dynamic_index_in_dim(askers, x, 3, keepdims=False)
    askers = lax.dynamic_index_in_dim(askers, core, 4, keepdims=False)[:, :, :RUN]
    askers = by_step(askers).reshape(NX * NC, RUN, HALF, 2) + rows
    givers = lax.dynamic_index_in_dim(full, x, 0, keepdims=False)
    givers = lax.dynamic_index_in_dim(givers, core, 1, keepdims=False)
    givers = lax.dynamic_index_in_dim(givers, z, 3, keepdims=False)[:, RUN:]
    givers = by_step(givers.transpose(2, 3, 1, 0)).reshape(NX * NC, CAP, HALF, 2)
    unused = jnp.full((NX * NC, KINDS - RUN - CAP, HALF, 2), -1, jnp.int32)
    sel = jnp.concatenate([askers, givers, unused], axis=1)
    offset = jnp.arange(2, dtype=jnp.int32) * (2 * rows)
    sel = jnp.where(sel >= 0, sel + offset, -1)
    sel = sel.transpose(2, 0, 3, 1).reshape(HALF, NX * NC * 2 * KINDS)

    ours = mine[RUN:].reshape(CAP, NX, NZ, NC).transpose(1, 3, 0, 2)
    ours = by_step(ours)
    ours = jnp.concatenate([ours, jnp.full((NX, NC, 1, NZ), -1, jnp.int32)], axis=2)
    theirs = lax.dynamic_index_in_dim(tables, me, 2, keepdims=False)
    theirs = by_step(theirs.reshape(NX, NZ, NC, RUN + CAP).transpose(0, 2, 3, 1))
    their_p = theirs[:, :, :RUN]
    their_q = theirs[:, :, RUN:]
    p_lanes = jnp.broadcast_to(ours[..., None], (NX, NC, RUN, NZ, RUN))
    q_lanes = jnp.where(
        their_q.transpose(0, 1, 3, 2)[:, :, None] >= 0, their_p[..., None] + rows, -1
    )
    pad = jnp.full((NX, NC, RUN, NZ, KINDS - RUN - CAP), -1, jnp.int32)
    meets = jnp.concatenate([p_lanes, q_lanes, pad], axis=-1)
    asked = jnp.concatenate(
        [
            jnp.full((NX, NC, NZ, RUN), -1, jnp.int32),
            their_q.transpose(0, 1, 3, 2),
            jnp.full((NX, NC, NZ, KINDS - RUN - CAP), -1, jnp.int32),
        ],
        axis=-1,
    )[:, :, None]
    idx = jnp.concatenate([meets, asked], axis=2).reshape(NX * NC, RUN + 1, NZ * KINDS)

    local = positives % rows
    ids = jnp.arange(rows, dtype=jnp.int32)
    of_passage = jnp.sum(jnp.where(local[:, None] == ids[None, :], ids[:, None], 0), axis=0)
    partner = jnp.concatenate([local + rows, of_passage])[None, :]

    grad_q, grad_p, loss = loss_grads(emb, w_full, sel, idx, partner)
    return (grad_q, grad_p, loss[0, :rows])


def solution(mesh):
    placed = (P("dp", "mp"), P("dp", "mp"), P("dp", "mp"), P("dp"), P("dp", None))
    return jax.shard_map(
        body,
        mesh=mesh,
        in_specs=placed,
        out_specs=(P("dp", "mp"), P("dp", "mp"), P("dp")),
        check_vma=False,
    )
```

```python
import functools

import jax
import jax.numpy as jnp
from jax import lax
from jax.experimental import pallas as pl
from jax.experimental.pallas import tpu as pltpu
from jax.sharding import PartitionSpec as P

SCALE = 20.0
EPS = 1e-06
MESH = pl.DeviceIdType.MESH
F32 = jnp.float32
BF16 = jnp.bfloat16

NX, NZ, NC, NY = 4, 16, 2, 4
NDP = NX * NZ * NC
NPEER = NX * NC
HALF = NZ // 2
RUN = 4
CAP = 3
LANES = 128
XFIRST = 384
KINDS = 8


def coords():
    dp = lax.axis_index("dp")
    y = lax.axis_index("mp")
    core = lax.rem(dp, NC)
    chip = lax.div(dp, NC)
    return lax.div(chip, NZ), y, lax.rem(chip, NZ), core


def dp_index(x, z, core):
    return (x * NZ + z) * NC + core


def wrap(value, size):
    return lax.rem(value + 2 * size, size)


def remote(src, dst, send_sem, recv_sem, dp, y):
    return pltpu.make_async_remote_copy(
        src_ref=src,
        dst_ref=dst,
        send_sem=send_sem,
        recv_sem=recv_sem,
        device_id=(dp, y),
        device_id_type=MESH,
    )


def nt(a, b):
    return lax.dot_general(a, b, (((1,), (1,)), ((), ())), preferred_element_type=F32)


def mm(a, b):
    return jnp.dot(a, b, preferred_element_type=F32)


def onehot(mask):
    return jnp.where(mask, 1.0, 0.0).astype(BF16)


def iota(shape, dim):
    return lax.broadcasted_iota(jnp.int32, shape, dim)


def down(mask, value):
    return jnp.sum(jnp.where(mask, value, 0.0), axis=0, keepdims=True)


def across(mask, value):
    return jnp.sum(jnp.where(mask, value, 0.0), axis=1, keepdims=True)


def greet(peers):
    barrier = pltpu.get_barrier_semaphore()
    for dp, y in peers:
        pl.semaphore_signal(barrier, inc=1, device_id=(dp, y), device_id_type=MESH)
    pl.semaphore_wait(barrier, len(peers))


def run_table(neg_ref, rows):
    holder = iota((rows, LANES), 1)
    query = iota((rows, LANES), 0).astype(F32)
    holder = dp_index(
        lax.div(holder, NZ * NC), lax.rem(holder, NZ), lax.rem(lax.div(holder, NZ), NC)
    )
    before = onehot(iota((rows, rows), 1) < iota((rows, rows), 0))
    base = jnp.zeros((1, LANES), F32)
    passages = [base] * RUN
    queries = [base] * CAP
    for r in range(neg_ref.shape[1] // RUN):
        first = neg_ref[:, RUN * r : RUN * r + 1]
        hit = lax.div(first, rows) == holder
        rank = mm(before, onehot(hit)) + base
        base = base + jnp.sum(jnp.where(hit, 1.0, 0.0), axis=0, keepdims=True)
        for i in range(CAP):
            queries[i] = queries[i] + down(hit & (rank == float(i)), query + 1.0)
        for j in range(RUN):
            local = lax.rem(neg_ref[:, RUN * r + j : RUN * r + j + 1], rows).astype(F32)
            named = jnp.max(jnp.where(hit, local, 0.0), axis=0, keepdims=True)
            passages[j] = jnp.maximum(passages[j], named)
    return jnp.concatenate(passages + [q - 1.0 for q in queries] + [jnp.full((1, LANES), -1.0)], 0)


def seen_z(z, step, second):
    ahead = jnp.where(step == 0, HALF, step)
    return lax.rem(jnp.where(second == 0, z - step + NZ, z + ahead), NZ)


def fill_tables(tab, sel_ref, idx_ref, rank, z, rows):
    lane8 = iota((NPEER, LANES), 1)
    row8 = iota((NPEER, LANES), 0)
    row = iota((LANES, LANES), 0)
    lane = iota((LANES, LANES), 1)
    kind = lax.rem(lane8, KINDS)
    second = lax.rem(lax.div(lane8, KINDS), 2)
    group = lax.div(lane8, 2 * KINDS)
    kind_l = lax.rem(lane, KINDS)
    second_l = lax.rem(lax.div(lane, KINDS), 2)
    group_l = lax.div(lane, 2 * KINDS)

    asked = jnp.concatenate([tab[d, z] for d in range(NPEER) for _ in range(2)], axis=0).astype(BF16)
    zero8 = jnp.zeros_like(row8)
    firsts = nt(onehot(lane8 == rank * NZ + seen_z(z, row8, zero8)), asked)
    seconds = nt(onehot(lane8 == rank * NZ + seen_z(z, row8, zero8 + 1)), asked)
    from_p = jnp.where(second == 0, firsts, seconds) + float(rows)
    here = tab[rank].reshape(LANES, LANES).astype(BF16)
    spread = mm(here, onehot(row == group_l * NZ + z))
    from_q = jnp.concatenate(
        [
            down(row == seen_z(z, jnp.full_like(lane, s), second_l) * KINDS + kind_l, spread)
            for s in range(HALF)
        ],
        axis=0,
    )
    picked = jnp.where(kind < RUN, from_p, from_q)
    picked = jnp.where(picked >= 0.0, picked + (second * 2 * rows).astype(F32), -1.0)
    sel_ref[...] = picked.astype(jnp.int32)

    z_l = seen_z(z, group_l, second_l)
    by_z = onehot(lax.rem(row, NZ) == z_l)
    mine = tab[rank, z]
    me_row = onehot(lane8 == rank * NZ + z)
    about_me = jnp.concatenate(
        [
            nt(me_row, tab[d].reshape(LANES, LANES).astype(BF16))[0:1] for d in range(NPEER)
        ],
        axis=0,
    ).astype(BF16)
    wants = mm(about_me, onehot(row == z_l * KINDS + kind_l))
    for r in range(RUN):
        own = jnp.where(lax.div(lane8, NZ) == row8, mine[RUN + r : RUN + r + 1], 0.0).astype(BF16)
        theirs = mm(about_me, onehot(row == z_l * KINDS + r)) + float(rows)
        theirs = jnp.where(wants >= 0.0, theirs, -1.0)
        idx_ref[r] = jnp.where(kind < RUN, mm(own, by_z), theirs).astype(jnp.int32)
    idx_ref[RUN] = jnp.where(kind < RUN, -1.0, wants).astype(jnp.int32)


def fused_kernel(
    hq_ref,
    hp_ref,
    w_ref,
    neg_ref,
    pos_ref,
    gq_ref,
    gp_ref,
    loss_ref,
    hid,
    wbuf,
    tab,
    sel_ref,
    idx_ref,
    col,
    outbox,
    recv,
    ybuf,
    dz,
    dtab,
    gpart,
    gin,
    acc,
    h_s,
    h_r,
    t_s,
    t_r,
    u_s,
    u_r,
    a_s,
    a_r,
    b_s,
    b_r,
    ax_s,
    ax_r,
    bx_s,
    bx_r,
    bd_s,
    bd_r,
    c_s,
    c_r,
    z_s,
    z_r,
    p_s,
    p_r,
    y_s,
    y_r,
    d_s,
    d_r,
    e_s,
    e_r,
    g_s,
    g_r,
):
    x, y, z, core = coords()
    me = dp_index(x, z, core)
    rank = x * NC + core
    rows, width = hq_ref.shape
    rows2 = 2 * rows
    half_w = width // 2
    depth = w_ref.shape[0]
    right = dp_index(x, wrap(z + 1, NZ), core)
    left = dp_index(x, wrap(z - 1, NZ), core)
    x_next = dp_index(wrap(x + 1, NX), z, core)
    x_prev = dp_index(wrap(x - 1, NX), z, core)
    sibling = dp_index(x, z, 1 - core)

    def peer_of(k):
        other = wrap(rank + k, NPEER)
        return dp_index(lax.div(other, NC), z, lax.rem(other, NC))

    y_peers = [wrap(y + k, NY) for k in range(1, NY)]
    z_peers = [dp_index(x, wrap(z + k, NZ), core) for k in range(1, NZ)]
    mates = [peer_of(k) for k in range(1, NPEER)]
    greet([(me, p) for p in y_peers] + [(p, y) for p in z_peers] + [(p, y) for p in mates])

    sent = []

    def send(src, dst, send_sem, recv_sem, dp, at_y):
        cp = remote(src, dst, send_sem, recv_sem, dp, at_y)
        cp.start()
        sent.append(cp)
        return cp

    def base_of(zb):
        return pl.multiple_of((zb * NC + core) * depth, depth)

    first_cols = pl.ds(0, XFIRST)
    other_cols = pl.ds(XFIRST, width - XFIRST)

    def a_block(zb, lo, count):
        return wbuf.at[pl.ds(lo, count), pl.ds(base_of(zb), depth), first_cols]

    def b_block(xb, zb, lo=0, count=depth):
        return wbuf.at[xb, pl.ds(pl.multiple_of(base_of(zb) + lo, count), count), other_cols]

    def z_of(block):
        if block <= HALF:
            return wrap(z - block, NZ)
        return wrap(z + block - HALF, NZ)

    def a_ring(direction, step):
        zb = wrap(z - (step - 1), NZ) if direction == 0 else wrap(z + (step - 1), NZ)
        part = a_block(zb, 0, NX) if step < HALF else a_block(zb, direction * (NX // 2), NX // 2)
        to = right if direction == 0 else left
        return send(part, part, a_s.at[direction, step - 1], a_r.at[direction, step - 1], to, y)

    def b_ring(direction, step):
        zb = wrap(z - (step - 1), NZ) if direction == 0 else wrap(z + (step - 1), NZ)
        if step < HALF:
            part = b_block(x, zb)
        else:
            part = b_block(x, zb, direction * (depth // 2), depth // 2)
        to = right if direction == 0 else left
        return send(part, part, b_s.at[direction, step - 1], b_r.at[direction, step - 1], to, y)

    def b_over_x(block):
        part = b_block(x, z_of(block))
        return [
            send(part, part, bx_s.at[way, block], bx_r.at[way, block], to, y)
            for way, to in ((0, x_next), (1, x_prev))
        ]

    def b_across(block, copies):
        out = []
        for way, to in ((0, x_next), (1, x_prev)):
            copies[way].wait_recv()
            xb = wrap(x - 1, NX) if way == 0 else wrap(x + 1, NX)
            part = b_block(xb, z_of(block), way * (depth // 2), depth // 2)
            out.append(send(part, part, bd_s.at[way, block], bd_r.at[way, block], to, y))
        return out

    def to_sibling(cols, which, block):
        part = wbuf.at[:, pl.ds(base_of(z_of(block)), depth), cols]
        return send(part, part, c_s.at[which, block], c_r.at[which, block], sibling, y)

    wbuf[x, pl.ds(base_of(z), depth), :] = w_ref[...]
    own_first = wbuf.at[x, pl.ds(base_of(z), depth), first_cols]
    a_over_x = [
        send(own_first, own_first, ax_s.at[k], ax_r.at[k], dp_index(wrap(x + k + 1, NX), z, core), y)
        for k in range(NX - 1)
    ]
    b_live = {(way, 1): b_ring(way, 1) for way in range(2)}
    over_x = {0: b_over_x(0)}
    hid[y, 0:rows, :] = hq_ref[...]
    hid[y, rows:rows2, :] = hp_ref[...]
    hidden = [
        send(hid.at[y], hid.at[y], h_s.at[k], h_r.at[k], me, peer) for k, peer in enumerate(y_peers)
    ]
    for cp in a_over_x:
        cp.wait_recv()
    a_live = {(way, 1): a_ring(way, 1) for way in range(2)}
    in_chip = [to_sibling(first_cols, 0, 0)]

    tab[rank, z] = run_table(neg_ref, rows)
    over_z = [
        send(tab.at[rank, z], tab.at[rank, z], t_s.at[k], t_r.at[k], peer, y)
        for k, peer in enumerate(z_peers)
    ]
    table_x = []

    across_x = {}
    blocks_of = {0: [0]}
    for step in range(1, HALF):
        blocks_of[step] = [step, HALF + step]
    blocks_of[HALF] = [HALF]

    def finish(step):
        for block in blocks_of[step]:
            for cp in across_x[block]:
                cp.wait_recv()
            in_chip.append(to_sibling(other_cols, 1, block))

    def turn(step):
        for block in blocks_of[step]:
            across_x[block] = b_across(block, over_x[block])

    for step in range(1, HALF + 1):
        for way in range(2):
            b_live[way, step].wait_recv()
            if step < HALF:
                b_live[way, step + 1] = b_ring(way, step + 1)
                over_x[blocks_of[step][way]] = b_over_x(blocks_of[step][way])
        if step == HALF:
            over_x[HALF] = b_over_x(HALF)
        for way in range(2):
            a_live[way, step].wait_recv()
            if step < HALF:
                a_live[way, step + 1] = a_ring(way, step + 1)
                in_chip.append(to_sibling(first_cols, 0, blocks_of[step][way]))
        if step == HALF:
            in_chip.append(to_sibling(first_cols, 0, HALF))
        turn(step - 1)
        if step > 1:
            finish(step - 2)
        if step == 2:
            for cp in over_z:
                cp.wait_recv()
            table_x = [
                send(tab.at[rank], tab.at[rank], u_s.at[k], u_r.at[k], peer, y)
                for k, peer in enumerate(mates)
            ]
        if step == HALF - 2:
            for cp in table_x:
                cp.wait_recv()
            fill_tables(tab, sel_ref, idx_ref, rank, z, rows)
    turn(HALF)
    finish(HALF - 1)
    finish(HALF)
    for cp in in_chip:
        cp.wait_recv()
    for cp in hidden:
        cp.wait_recv()

    tile = 256

    @pl.loop(0, width // tile)
    def _(t):
        cols = pl.ds(pl.multiple_of(t * tile, tile), tile)
        total = jnp.zeros((rows2, tile), F32)
        for b in range(NY):
            total = total + mm(hid[b], wbuf[b, :, cols])
        col[0, 0:rows2, cols] = total.astype(BF16)

    def ring(direction, step, piece):
        src_at = piece * rows if direction == 0 or step == 1 else rows2 + piece * rows
        if step < HALF:
            src = col.at[step - 1, pl.ds(src_at, rows)]
            dst = col.at[step, pl.ds(direction * rows2 + piece * rows, rows)]
        else:
            cols = pl.ds(direction * half_w, half_w)
            src = col.at[step - 1, pl.ds(src_at, rows), cols]
            dst = col.at[0, pl.ds(rows2 + piece * rows, rows), cols]
        to = right if direction == 0 else left
        send_sem = z_s.at[direction, step - 1, piece]
        return send(src, dst, send_sem, z_r.at[direction, step - 1, piece], to, y)

    live = {}
    for piece in range(2):
        for direction in range(2):
            live[direction, 1, piece] = ring(direction, 1, piece)

    pair_rows = iota((2 * rows2, LANES), 0)
    passed = []
    for step in range(1, HALF + 1):
        for piece in range(2):
            for direction in range(2):
                live[direction, step, piece].wait_recv()
                if step < HALF:
                    live[direction, step + 1, piece] = ring(direction, step + 1, piece)
        slot = step % HALF
        pick = onehot(pair_rows == sel_ref[slot : slot + 1, :])
        picked = lax.dot_general(
            pick, col[slot], (((0,), (0,)), ((), ())), preferred_element_type=F32
        )
        outbox[slot] = picked.astype(BF16).reshape(NPEER, 2 * KINDS, width)
        for k, peer in enumerate(mates):
            src = outbox.at[slot, wrap(rank + k + 1, NPEER)]
            passed.append(
                send(src, recv.at[rank, slot], p_s.at[slot, k], p_r.at[slot, k], peer, y)
            )
        recv[rank, slot] = outbox[slot, rank]

    lane = iota((1, rows2), 1)
    row_id = iota((rows2, rows2), 0)
    lane_id = iota((rows2, rows2), 1)
    eye = row_id == lane_id
    emb = col[0, 0:rows2, :]
    local = lax.rem(pos_ref[...], rows)
    partner = jnp.concatenate([local, local], axis=1).astype(F32)
    partner_col = across(eye, partner).astype(jnp.int32)
    partner = partner.astype(jnp.int32)
    pair = ((lane_id < rows) & (row_id == partner + rows)) | (
        (row_id < rows) & (lane_id == partner_col + rows)
    )

    def mask_of(d, r):
        return row_id == idx_ref[r, d : d + 1, :]

    gram = nt(emb, emb)
    own_sq = down(eye, gram)
    own_pos = down(pair, gram)
    for cp in passed:
        cp.wait_recv()
    for d in range(NPEER):
        got = recv[d].reshape(rows2, width)
        cross = nt(emb, got)
        parts = [down(mask_of(d, r), cross) for r in range(RUN)]
        parts += [down(eye, nt(got, got)), own_sq, own_pos, jnp.zeros_like(own_sq)]
        ybuf[y, d] = jnp.concatenate(parts, axis=0)
    over_y = [
        send(ybuf.at[y], ybuf.at[y], y_s.at[k], y_r.at[k], me, peer) for k, peer in enumerate(y_peers)
    ]
    for cp in over_y:
        cp.wait_recv()

    sums = [((ybuf[0, d] + ybuf[1, d]) + ybuf[2, d]) + ybuf[3, d] for d in range(NPEER)]
    inv_row = 1.0 / jnp.sqrt(sums[0][5:6] + EPS)
    inv_col = across(eye, inv_row)
    pos_score = SCALE * sums[0][6:7] * inv_row * down(pair, inv_col)
    pos_exp = jnp.exp(pos_score)
    denom = across(eye, pos_exp)
    scores = []
    exps = []
    lane_inv = []
    for d in range(NPEER):
        rl = 1.0 / jnp.sqrt(sums[d][4:5] + EPS)
        lane_inv.append(rl)
        sc = []
        ex = []
        for r in range(RUN):
            mask = mask_of(d, r)
            s = SCALE * sums[d][r : r + 1] * rl * down(mask, inv_col)
            e = jnp.exp(s)
            sc.append(s)
            ex.append(e)
            denom = denom + across(mask, e)
        scores.append(sc)
        exps.append(ex)
    denom_row = down(eye, denom)
    loss_ref[...] = jnp.log(denom_row[:, 0:rows]) - pos_score[:, 0:rows]
    is_query = lane < rows
    dinv_row = jnp.where(is_query, 1.0 / denom_row, 0.0)
    dinv_col = across(eye, dinv_row)

    dz[0] = dinv_row
    inv_z = [
        send(dz.at[0], dz.at[k + 1], d_s.at[k], d_r.at[k], peer, y) for k, peer in enumerate(z_peers)
    ]

    pos_coef = jnp.where(is_query, SCALE * (pos_exp * dinv_row - 1.0), 0.0)
    pos_coef = pos_coef + down(pair, across(eye, pos_coef))

    def half_grads(part, dinv_at):
        rows_at = slice(part * rows, (part + 1) * rows)
        half_id = iota((rows, rows2), 0) + part * rows

        def add_rows(weights, values, fresh=False):
            high = weights.astype(BF16)
            low = (weights - high.astype(F32)).astype(BF16)
            term = mm(jnp.concatenate([high, low], axis=0), values)
            term = term[0:rows] + term[rows:]
            acc[...] = term if fresh else acc[...] + term

        half_pair = pair[rows_at]
        add_rows(jnp.where(half_pair, pos_coef * inv_row, 0.0), emb, True)
        inner = across(half_pair, pos_coef * pos_score * (1.0 / SCALE))
        for d in range(NPEER):
            weights = jnp.zeros((rows, rows2), F32)
            for r in range(RUN):
                mask = half_id == idx_ref[r, d : d + 1, :]
                coef = SCALE * exps[d][r] * dinv_at(d, r)
                weights = weights + jnp.where(mask, coef * lane_inv[d], 0.0)
                inner = inner + across(mask, coef * scores[d][r] * (1.0 / SCALE))
            add_rows(weights, recv[d].reshape(rows2, width))
        unit = emb[rows_at].astype(F32) * inv_col[rows_at]
        return ((acc[...] - unit * inner) * inv_col[rows_at]).astype(BF16)

    def project(part, g_emb):
        copies = []
        for k in range(1, NY + 1):
            block = wrap(y + k, NY)
            gpart[part, k - 1] = nt(g_emb, wbuf[block]).astype(BF16)
            if k < NY:
                mine = gpart.at[part, k - 1]
                theirs = gin.at[part, k - 1]
                copies.append(
                    send(mine, theirs, g_s.at[part, k - 1], g_r.at[part, k - 1], me, block)
                )
        return copies

    def gathered(part, copies):
        total = gpart[part, NY - 1].astype(F32)
        for k, cp in enumerate(copies):
            cp.wait_recv()
            total = total + gin[part, k].astype(F32)
        return total.astype(BF16)

    g_query = half_grads(0, lambda d, r: down(mask_of(d, r), dinv_col))
    for cp in inv_z:
        cp.wait_recv()
    inv_x = [
        send(dz, dtab.at[k + 1], e_s.at[k], e_r.at[k], peer, y) for k, peer in enumerate(mates)
    ]
    for k in range(NZ):
        dtab[0, k] = dz[k]
    q_copies = project(0, g_query)

    for cp in inv_x:
        cp.wait_recv()
    place = iota((NZ, rows2), 0)
    lane16 = iota((NZ, rows2), 1)
    step16 = lax.div(lane16, 2 * KINDS)
    second16 = lax.rem(lax.div(lane16, KINDS), 2)
    source = jnp.where(second16 == 0, step16, jnp.where(step16 == 0, HALF, NZ - step16))
    at_source = place == source
    their_inv = []
    for d in range(NPEER):
        table = jnp.concatenate([dtab[wrap(rank - d, NPEER), k] for k in range(NZ)], axis=0)
        spread = jnp.where(row_id == idx_ref[RUN, d : d + 1, :], 1.0, 0.0)
        found = jnp.dot(table, spread, preferred_element_type=F32, precision=lax.Precision.HIGHEST)
        their_inv.append(down(at_source, found))
    p_copies = project(1, half_grads(1, lambda d, r: their_inv[d]))
    gq_ref[...] = gathered(0, q_copies)
    gp_ref[...] = gathered(1, p_copies)
    for cp in sent:
        cp.wait_send()


def body(q_hidden, p_hidden, proj, positives, negatives):
    rows, width = q_hidden.shape
    rows2 = 2 * rows
    block = proj.shape[0] * NDP // NX
    vmem = pl.BlockSpec(memory_space=pltpu.VMEM)
    dma = pltpu.SemaphoreType.DMA

    def both(*shape):
        return [dma(shape), dma(shape)]

    grad_q, grad_p, loss = pl.pallas_call(
        fused_kernel,
        out_shape=(
            jax.ShapeDtypeStruct((rows, width), BF16),
            jax.ShapeDtypeStruct((rows, width), BF16),
            jax.ShapeDtypeStruct((1, rows), F32),
        ),
        in_specs=[vmem] * 5,
        out_specs=(vmem,) * 3,
        scratch_shapes=[
            pltpu.VMEM((NY, rows2, width), BF16),
            pltpu.VMEM((NX, block, width), BF16),
            pltpu.VMEM((NPEER, NZ, 8, LANES), F32),
            pltpu.VMEM((HALF, LANES), jnp.int32),
            pltpu.VMEM((RUN + 1, NPEER, LANES), jnp.int32),
            pltpu.VMEM((HALF, 2 * rows2, width), BF16),
            pltpu.VMEM((HALF, NPEER, 2 * KINDS, width), BF16),
            pltpu.VMEM((NPEER, HALF, 2 * KINDS, width), BF16),
            pltpu.VMEM((NY, NPEER, 8, rows2), F32),
            pltpu.VMEM((NZ, 1, rows2), F32),
            pltpu.VMEM((NPEER, NZ, 1, rows2), F32),
            pltpu.VMEM((2, NY, rows, width), BF16),
            pltpu.VMEM((2, NY - 1, rows, width), BF16),
            pltpu.VMEM((rows, width), F32),
        ]
        + both(NY - 1)
        + both(NZ - 1)
        + both(NPEER - 1)
        + both(2, HALF)
        + both(2, HALF)
        + both(NX - 1)
        + both(2, NZ)
        + both(2, NZ)
        + both(2, NZ)
        + both(2, HALF, 2)
        + both(HALF, NPEER - 1)
        + both(NY - 1)
        + both(NZ - 1)
        + both(NPEER - 1)
        + both(2, NY - 1),
        compiler_params=pltpu.CompilerParams(
            collective_id=0, has_side_effects=True, vmem_limit_bytes=56 * 1024 * 1024
        ),
        cost_estimate=pl.CostEstimate(
            flops=3 * 10**9, bytes_accessed=10**8, transcendentals=10**5
        ),
        name="contrastive_backward",
    )(q_hidden, p_hidden, proj, negatives, positives[None, :])
    return (grad_q, grad_p, loss[0])


def solution(mesh):
    placed = (P("dp", "mp"), P("dp", "mp"), P("dp", "mp"), P("dp"), P("dp", None))
    return jax.shard_map(
        body,
        mesh=mesh,
        in_specs=placed,
        out_specs=(P("dp", "mp"), P("dp", "mp"), P("dp")),
        check_vma=False,
    )
```

```python
import functools

import jax
import jax.numpy as jnp
from jax import lax
from jax.experimental import pallas as pl
from jax.experimental.pallas import tpu as pltpu
from jax.sharding import PartitionSpec as P

SCALE = 20.0
EPS = 1e-06
MESH = pl.DeviceIdType.MESH
F32 = jnp.float32
BF16 = jnp.bfloat16

NX, NZ, NC, NY = 4, 16, 2, 4
NDP = NX * NZ * NC
NPEER = NX * NC
HALF = NZ // 2
RUN = 4
CAP = 3
LANES = 128
XFIRST = 384
APARTS = 4
EPARTS = 4
KINDS = 8


def coords():
    dp = lax.axis_index("dp")
    y = lax.axis_index("mp")
    core = lax.rem(dp, NC)
    chip = lax.div(dp, NC)
    return lax.div(chip, NZ), y, lax.rem(chip, NZ), core


def dp_index(x, z, core):
    return (x * NZ + z) * NC + core


def wrap(value, size):
    return lax.rem(value + 2 * size, size)


def remote(src, dst, send_sem, recv_sem, dp, y):
    return pltpu.make_async_remote_copy(
        src_ref=src,
        dst_ref=dst,
        send_sem=send_sem,
        recv_sem=recv_sem,
        device_id=(dp, y),
        device_id_type=MESH,
    )


def nt(a, b):
    return lax.dot_general(a, b, (((1,), (1,)), ((), ())), preferred_element_type=F32)


def mm(a, b):
    return jnp.dot(a, b, preferred_element_type=F32)


def onehot(mask):
    return jnp.where(mask, 1.0, 0.0).astype(BF16)


def iota(shape, dim):
    return lax.broadcasted_iota(jnp.int32, shape, dim)


def down(mask, value):
    return jnp.sum(jnp.where(mask, value, 0.0), axis=0, keepdims=True)


def across(mask, value):
    return jnp.sum(jnp.where(mask, value, 0.0), axis=1, keepdims=True)


def greet(peers):
    barrier = pltpu.get_barrier_semaphore()
    for dp, y in peers:
        pl.semaphore_signal(barrier, inc=1, device_id=(dp, y), device_id_type=MESH)
    pl.semaphore_wait(barrier, len(peers))


def run_table(neg_ref, rows):
    holder = iota((rows, LANES), 1)
    query = iota((rows, LANES), 0).astype(F32)
    holder = dp_index(
        lax.div(holder, NZ * NC), lax.rem(holder, NZ), lax.rem(lax.div(holder, NZ), NC)
    ).astype(F32)
    before = onehot(iota((rows, rows), 1) < iota((rows, rows), 0))
    base = jnp.zeros((1, LANES), F32)
    passages = [base] * RUN
    queries = [base] * CAP
    ids = neg_ref[...]
    turn = onehot(iota((rows, rows), 0) == iota((rows, rows), 1))
    owners = nt(turn, lax.div(ids, rows).astype(F32).astype(BF16))
    locals_ = nt(turn, lax.rem(ids, rows).astype(F32).astype(BF16))
    for r in range(neg_ref.shape[0] // RUN):
        hit = owners[:, RUN * r : RUN * r + 1] == holder
        rank = mm(before, onehot(hit)) + base
        base = base + jnp.sum(jnp.where(hit, 1.0, 0.0), axis=0, keepdims=True)
        for i in range(CAP):
            queries[i] = queries[i] + down(hit & (rank == float(i)), query + 1.0)
        for j in range(RUN):
            local = locals_[:, RUN * r + j : RUN * r + j + 1]
            named = jnp.max(jnp.where(hit, local, 0.0), axis=0, keepdims=True)
            passages[j] = jnp.maximum(passages[j], named)
    return jnp.concatenate(passages + [q - 1.0 for q in queries] + [jnp.full((1, LANES), -1.0)], 0)


def seen_z(z, step, second):
    ahead = jnp.where(step == 0, HALF, step)
    return lax.rem(jnp.where(second == 0, z - step + NZ, z + ahead), NZ)


def fill_tables(tab, sel_ref, idx_ref, rank, z, rows):
    lane8 = iota((NPEER, LANES), 1)
    row8 = iota((NPEER, LANES), 0)
    row = iota((LANES, LANES), 0)
    lane = iota((LANES, LANES), 1)
    kind = lax.rem(lane8, KINDS)
    second = lax.rem(lax.div(lane8, KINDS), 2)
    group = lax.div(lane8, 2 * KINDS)
    kind_l = lax.rem(lane, KINDS)
    second_l = lax.rem(lax.div(lane, KINDS), 2)
    group_l = lax.div(lane, 2 * KINDS)

    asked = jnp.concatenate([tab[d, z] for d in range(NPEER) for _ in range(2)], axis=0).astype(BF16)
    zero8 = jnp.zeros_like(row8)
    firsts = nt(onehot(lane8 == rank * NZ + seen_z(z, row8, zero8)), asked)
    seconds = nt(onehot(lane8 == rank * NZ + seen_z(z, row8, zero8 + 1)), asked)
    from_p = jnp.where(second == 0, firsts, seconds) + float(rows)
    here = tab[rank].reshape(LANES, LANES).astype(BF16)
    spread = mm(here, onehot(row == group_l * NZ + z))
    from_q = jnp.concatenate(
        [
            down(row == seen_z(z, jnp.full_like(lane, s), second_l) * KINDS + kind_l, spread)
            for s in range(HALF)
        ],
        axis=0,
    )
    picked = jnp.where(kind < RUN, from_p, from_q)
    picked = jnp.where(picked >= 0.0, picked + (second * 2 * rows).astype(F32), -1.0)
    sel_ref[...] = picked.astype(jnp.int32)

    z_l = seen_z(z, group_l, second_l)
    by_z = onehot(lax.rem(row, NZ) == z_l)
    mine = tab[rank, z]
    me_row = onehot(lane8 == rank * NZ + z)
    about_me = jnp.concatenate(
        [
            nt(me_row, tab[d].reshape(LANES, LANES).astype(BF16))[0:1] for d in range(NPEER)
        ],
        axis=0,
    ).astype(BF16)
    wants = mm(about_me, onehot(row == z_l * KINDS + kind_l))
    for r in range(RUN):
        own = jnp.where(lax.div(lane8, NZ) == row8, mine[RUN + r : RUN + r + 1], 0.0).astype(BF16)
        theirs = mm(about_me, onehot(row == z_l * KINDS + r)) + float(rows)
        theirs = jnp.where(wants >= 0.0, theirs, -1.0)
        idx_ref[r] = jnp.where(kind < RUN, mm(own, by_z), theirs).astype(jnp.int32)
    idx_ref[RUN] = jnp.where(kind < RUN, -1.0, wants).astype(jnp.int32)


def fused_kernel(
    hq_ref,
    hp_ref,
    w_ref,
    neg_ref,
    pos_ref,
    gq_ref,
    gp_ref,
    loss_ref,
    hid,
    wbuf,
    tab,
    sel_ref,
    idx_ref,
    col,
    outbox,
    recv,
    ybuf,
    dz,
    dtab,
    gpart,
    gin,
    acc,
    h_s,
    h_r,
    t_s,
    t_r,
    u_s,
    u_r,
    a_s,
    a_r,
    b_s,
    b_r,
    ax_s,
    ax_r,
    bx_s,
    bx_r,
    bd_s,
    bd_r,
    c_s,
    c_r,
    z_s,
    z_r,
    p_s,
    p_r,
    y_s,
    y_r,
    d_s,
    d_r,
    e_s,
    e_r,
    g_s,
    g_r,
):
    x, y, z, core = coords()
    me = dp_index(x, z, core)
    rank = x * NC + core
    rows, width = hq_ref.shape
    rows2 = 2 * rows
    depth = w_ref.shape[0]
    right = dp_index(x, wrap(z + 1, NZ), core)
    left = dp_index(x, wrap(z - 1, NZ), core)
    x_next = dp_index(wrap(x + 1, NX), z, core)
    x_prev = dp_index(wrap(x - 1, NX), z, core)
    sibling = dp_index(x, z, 1 - core)

    def peer_of(k):
        other = wrap(rank + k, NPEER)
        return dp_index(lax.div(other, NC), z, lax.rem(other, NC))

    y_peers = [wrap(y + k, NY) for k in range(1, NY)]
    z_peers = [dp_index(x, wrap(z + k, NZ), core) for k in range(1, NZ)]
    mates = [peer_of(k) for k in range(1, NPEER)]
    greet([(me, p) for p in y_peers] + [(right, y), (left, y)] + [(p, y) for p in mates])

    sent = []

    def send(src, dst, send_sem, recv_sem, dp, at_y):
        cp = remote(src, dst, send_sem, recv_sem, dp, at_y)
        cp.start()
        sent.append(cp)
        return cp

    def base_of(zb):
        return pl.multiple_of((zb * NC + core) * depth, depth)

    first_cols = pl.ds(0, XFIRST)
    other_cols = pl.ds(XFIRST, width - XFIRST)

    def a_block(zb, lo, count):
        return wbuf.at[pl.ds(lo, count), pl.ds(base_of(zb), depth), first_cols]

    def b_block(xb, zb, lo=0, count=depth):
        return wbuf.at[xb, pl.ds(pl.multiple_of(base_of(zb) + lo, count), count), other_cols]

    def z_of(block):
        if block <= HALF:
            return wrap(z - block, NZ)
        return wrap(z + block - HALF, NZ)

    def a_ring(direction, step, piece):
        zb = wrap(z - (step - 1), NZ) if direction == 0 else wrap(z + (step - 1), NZ)
        part = a_block(zb, piece * (NX // APARTS), NX // APARTS)
        to = right if direction == 0 else left
        at = (direction, step - 1, piece)
        return send(part, part, a_s.at[at], a_r.at[at], to, y)

    def t_ring(direction, step):
        zb = wrap(z - (step - 1), NZ) if direction == 0 else wrap(z + (step - 1), NZ)
        part = tab.at[rank, zb]
        to = right if direction == 0 else left
        return send(part, part, t_s.at[direction, step - 1], t_r.at[direction, step - 1], to, y)

    def b_ring(direction, step):
        zb = wrap(z - (step - 1), NZ) if direction == 0 else wrap(z + (step - 1), NZ)
        if step < HALF:
            part = b_block(x, zb)
        else:
            part = b_block(x, zb, direction * (depth // 2), depth // 2)
        to = right if direction == 0 else left
        return send(part, part, b_s.at[direction, step - 1], b_r.at[direction, step - 1], to, y)

    def b_over_x(block):
        part = b_block(x, z_of(block))
        return [
            send(part, part, bx_s.at[way, block], bx_r.at[way, block], to, y)
            for way, to in ((0, x_next), (1, x_prev))
        ]

    def b_across(block, copies):
        out = []
        for way, to in ((0, x_next), (1, x_prev)):
            copies[way].wait_recv()
            xb = wrap(x - 1, NX) if way == 0 else wrap(x + 1, NX)
            part = b_block(xb, z_of(block), way * (depth // 2), depth // 2)
            out.append(send(part, part, bd_s.at[way, block], bd_r.at[way, block], to, y))
        return out

    def to_sibling(cols, which, block):
        part = wbuf.at[:, pl.ds(base_of(z_of(block)), depth), cols]
        return send(part, part, c_s.at[which, block], c_r.at[which, block], sibling, y)

    wbuf[x, pl.ds(base_of(z), depth), :] = w_ref[...]
    own_first = wbuf.at[x, pl.ds(base_of(z), depth), first_cols]
    a_over_x = [
        send(own_first, own_first, ax_s.at[k], ax_r.at[k], dp_index(wrap(x + k + 1, NX), z, core), y)
        for k in range(NX - 1)
    ]
    b_live = {(way, 1): b_ring(way, 1) for way in range(2)}
    over_x = {0: b_over_x(0)}
    hid[y, 0:rows, :] = hq_ref[...]
    hid[y, rows:rows2, :] = hp_ref[...]
    hidden = [
        send(hid.at[y], hid.at[y], h_s.at[k], h_r.at[k], me, peer) for k, peer in enumerate(y_peers)
    ]
    for cp in a_over_x:
        cp.wait_recv()
    a_live = {}
    for piece in range(APARTS):
        for way in range(2):
            a_live[way, 1, piece] = a_ring(way, 1, piece)
    in_chip = [to_sibling(first_cols, 0, 0)]

    tab[rank, z] = run_table(neg_ref, rows)
    t_live = {(way, 1): t_ring(way, 1) for way in range(2)}

    across_x = {}
    blocks_of = {0: [0]}
    for step in range(1, HALF):
        blocks_of[step] = [step, HALF + step]
    blocks_of[HALF] = [HALF]

    def finish(step):
        for block in blocks_of[step]:
            for cp in across_x[block]:
                cp.wait_recv()
            in_chip.append(to_sibling(other_cols, 1, block))

    def turn(step):
        for block in blocks_of[step]:
            across_x[block] = b_across(block, over_x[block])

    for step in range(1, HALF + 1):
        for way in range(2):
            b_live[way, step].wait_recv()
            if step < HALF:
                b_live[way, step + 1] = b_ring(way, step + 1)
                over_x[blocks_of[step][way]] = b_over_x(blocks_of[step][way])
        if step == HALF:
            over_x[HALF] = b_over_x(HALF)
        for piece in range(APARTS):
            for way in range(2):
                if (way, step, piece) not in a_live:
                    continue
                a_live[way, step, piece].wait_recv()
                if step + 1 < HALF or (step + 1 == HALF and piece * 2 // APARTS == way):
                    a_live[way, step + 1, piece] = a_ring(way, step + 1, piece)
        for way in range(2):
            if (way, step) in t_live:
                t_live[way, step].wait_recv()
                if step + 1 < HALF or (step + 1 == HALF and way == 0):
                    t_live[way, step + 1] = t_ring(way, step + 1)
        for block in blocks_of[step]:
            in_chip.append(to_sibling(first_cols, 0, block))
        if step > 1:
            turn(step - 2)
        if step > 3:
            finish(step - 4)
    table_x = [
        send(tab.at[rank], tab.at[rank], u_s.at[k], u_r.at[k], peer, y)
        for k, peer in enumerate(mates)
    ]
    turn(HALF - 1)
    finish(HALF - 3)
    turn(HALF)
    finish(HALF - 2)
    finish(HALF - 1)
    finish(HALF)
    for cp in in_chip:
        cp.wait_recv()
    for cp in hidden:
        cp.wait_recv()

    tile = width // EPARTS

    def ring(direction, step, piece):
        src_at = 0 if direction == 0 or step == 1 else rows2
        cols = pl.ds(piece * tile, tile)
        src = col.at[step - 1, pl.ds(src_at, rows2), cols]
        if step < HALF:
            dst = col.at[step, pl.ds(direction * rows2, rows2), cols]
        else:
            dst = col.at[0, pl.ds(rows2, rows2), cols]
        to = right if direction == 0 else left
        at = (direction, step - 1, piece)
        return send(src, dst, z_s.at[at], z_r.at[at], to, y)

    live = {}
    for piece in range(EPARTS):
        total = jnp.zeros((rows2, tile), F32)
        for b in range(NY):
            total = total + mm(hid[b], wbuf[b, :, piece * tile : (piece + 1) * tile])
        col[0, 0:rows2, piece * tile : (piece + 1) * tile] = total.astype(BF16)
        for direction in range(2):
            live[direction, 1, piece] = ring(direction, 1, piece)
    for cp in table_x:
        cp.wait_recv()
    fill_tables(tab, sel_ref, idx_ref, rank, z, rows)

    pair_rows = iota((2 * rows2, LANES), 0)
    passed = []
    for step in range(1, HALF + 1):
        for piece in range(EPARTS):
            for direction in range(2):
                if (direction, step, piece) not in live:
                    continue
                live[direction, step, piece].wait_recv()
                if step + 1 < HALF or (step + 1 == HALF and piece * 2 // EPARTS == direction):
                    live[direction, step + 1, piece] = ring(direction, step + 1, piece)
        slot = step % HALF
        pick = onehot(pair_rows == sel_ref[slot : slot + 1, :])
        picked = lax.dot_general(
            pick, col[slot], (((0,), (0,)), ((), ())), preferred_element_type=F32
        )
        outbox[slot] = picked.astype(BF16).reshape(NPEER, 2 * KINDS, width)
        for k, peer in enumerate(mates):
            src = outbox.at[slot, wrap(rank + k + 1, NPEER)]
            passed.append(
                send(src, recv.at[rank, slot], p_s.at[slot, k], p_r.at[slot, k], peer, y)
            )
        recv[rank, slot] = outbox[slot, rank]

    lane = iota((1, rows2), 1)
    row_id = iota((rows2, rows2), 0)
    lane_id = iota((rows2, rows2), 1)
    eye = row_id == lane_id
    emb = col[0, 0:rows2, :]
    local = lax.rem(pos_ref[...], rows)
    partner = jnp.concatenate([local, local], axis=1).astype(F32)
    partner_col = across(eye, partner).astype(jnp.int32)
    partner = partner.astype(jnp.int32)
    pair = ((lane_id < rows) & (row_id == partner + rows)) | (
        (row_id < rows) & (lane_id == partner_col + rows)
    )

    def mask_of(d, r):
        return row_id == idx_ref[r, d : d + 1, :]

    gram = nt(emb, emb)
    own_sq = down(eye, gram)
    own_pos = down(pair, gram)
    for cp in passed:
        cp.wait_recv()
    for d in range(NPEER):
        got = recv[d].reshape(rows2, width)
        cross = nt(emb, got)
        parts = [down(mask_of(d, r), cross) for r in range(RUN)]
        parts += [down(eye, nt(got, got)), own_sq, own_pos, jnp.zeros_like(own_sq)]
        ybuf[y, d] = jnp.concatenate(parts, axis=0)
    over_y = [
        send(ybuf.at[y], ybuf.at[y], y_s.at[k], y_r.at[k], me, peer) for k, peer in enumerate(y_peers)
    ]
    for cp in over_y:
        cp.wait_recv()

    sums = [((ybuf[0, d] + ybuf[1, d]) + ybuf[2, d]) + ybuf[3, d] for d in range(NPEER)]
    inv_row = 1.0 / jnp.sqrt(sums[0][5:6] + EPS)
    inv_col = across(eye, inv_row)
    pos_score = SCALE * sums[0][6:7] * inv_row * down(pair, inv_col)
    pos_exp = jnp.exp(pos_score)
    denom = across(eye, pos_exp)
    scores = []
    exps = []
    lane_inv = []
    for d in range(NPEER):
        rl = 1.0 / jnp.sqrt(sums[d][4:5] + EPS)
        lane_inv.append(rl)
        sc = []
        ex = []
        for r in range(RUN):
            mask = mask_of(d, r)
            s = SCALE * sums[d][r : r + 1] * rl * down(mask, inv_col)
            e = jnp.exp(s)
            sc.append(s)
            ex.append(e)
            denom = denom + across(mask, e)
        scores.append(sc)
        exps.append(ex)
    denom_row = down(eye, denom)
    loss_ref[...] = jnp.log(denom_row[:, 0:rows]) - pos_score[:, 0:rows]
    is_query = lane < rows
    dinv_row = jnp.where(is_query, 1.0 / denom_row, 0.0)
    dinv_col = across(eye, dinv_row)

    dz[0] = dinv_row
    inv_z = [
        send(dz.at[0], dz.at[k + 1], d_s.at[k], d_r.at[k], peer, y) for k, peer in enumerate(z_peers)
    ]

    pos_coef = jnp.where(is_query, SCALE * (pos_exp * dinv_row - 1.0), 0.0)
    pos_coef = pos_coef + down(pair, across(eye, pos_coef))

    def half_grads(part, dinv_at):
        rows_at = slice(part * rows, (part + 1) * rows)
        half_id = iota((rows, rows2), 0) + part * rows

        def add_rows(weights, values, fresh=False):
            high = weights.astype(BF16)
            low = (weights - high.astype(F32)).astype(BF16)
            term = mm(jnp.concatenate([high, low], axis=0), values)
            term = term[0:rows] + term[rows:]
            acc[...] = term if fresh else acc[...] + term

        half_pair = pair[rows_at]
        add_rows(jnp.where(half_pair, pos_coef * inv_row, 0.0), emb, True)
        inner = across(half_pair, pos_coef * pos_score * (1.0 / SCALE))
        for d in range(NPEER):
            weights = jnp.zeros((rows, rows2), F32)
            for r in range(RUN):
                mask = half_id == idx_ref[r, d : d + 1, :]
                coef = SCALE * exps[d][r] * dinv_at(d, r)
                weights = weights + jnp.where(mask, coef * lane_inv[d], 0.0)
                inner = inner + across(mask, coef * scores[d][r] * (1.0 / SCALE))
            add_rows(weights, recv[d].reshape(rows2, width))
        unit = emb[rows_at].astype(F32) * inv_col[rows_at]
        return ((acc[...] - unit * inner) * inv_col[rows_at]).astype(BF16)

    def project(part, g_emb):
        copies = []
        for k in (2, 1, 3, NY):
            block = wrap(y + k, NY)
            gpart[part, k - 1] = nt(g_emb, wbuf[block]).astype(BF16)
            if k < NY:
                mine = gpart.at[part, k - 1]
                theirs = gin.at[part, k - 1]
                copies.append(
                    send(mine, theirs, g_s.at[part, k - 1], g_r.at[part, k - 1], me, block)
                )
        return copies

    def gathered(part, copies):
        total = gpart[part, NY - 1].astype(F32)
        for cp in copies:
            cp.wait_recv()
        for k in range(NY - 1):
            total = total + gin[part, k].astype(F32)
        return total.astype(BF16)

    g_query = half_grads(0, lambda d, r: down(mask_of(d, r), dinv_col))
    for cp in inv_z:
        cp.wait_recv()
    inv_x = [
        send(dz, dtab.at[k + 1], e_s.at[k], e_r.at[k], peer, y) for k, peer in enumerate(mates)
    ]
    for k in range(NZ):
        dtab[0, k] = dz[k]
    q_copies = project(0, g_query)

    for cp in inv_x:
        cp.wait_recv()
    place = iota((NZ, rows2), 0)
    lane16 = iota((NZ, rows2), 1)
    step16 = lax.div(lane16, 2 * KINDS)
    second16 = lax.rem(lax.div(lane16, KINDS), 2)
    source = jnp.where(second16 == 0, step16, jnp.where(step16 == 0, HALF, NZ - step16))
    at_source = place == source
    their_inv = []
    for d in range(NPEER):
        table = jnp.concatenate([dtab[wrap(rank - d, NPEER), k] for k in range(NZ)], axis=0)
        spread = jnp.where(row_id == idx_ref[RUN, d : d + 1, :], 1.0, 0.0)
        found = jnp.dot(table, spread, preferred_element_type=F32, precision=lax.Precision.HIGHEST)
        their_inv.append(down(at_source, found))
    p_copies = project(1, half_grads(1, lambda d, r: their_inv[d]))
    gq_ref[...] = gathered(0, q_copies)
    gp_ref[...] = gathered(1, p_copies)
    for cp in sent:
        cp.wait_send()


def body(q_hidden, p_hidden, proj, positives, negatives):
    rows, width = q_hidden.shape
    rows2 = 2 * rows
    block = proj.shape[0] * NDP // NX
    vmem = pl.BlockSpec(memory_space=pltpu.VMEM)
    dma = pltpu.SemaphoreType.DMA

    def both(*shape):
        return [dma(shape), dma(shape)]

    grad_q, grad_p, loss = pl.pallas_call(
        fused_kernel,
        out_shape=(
            jax.ShapeDtypeStruct((rows, width), BF16),
            jax.ShapeDtypeStruct((rows, width), BF16),
            jax.ShapeDtypeStruct((1, rows), F32),
        ),
        in_specs=[vmem] * 5,
        out_specs=(vmem,) * 3,
        scratch_shapes=[
            pltpu.VMEM((NY, rows2, width), BF16),
            pltpu.VMEM((NX, block, width), BF16),
            pltpu.VMEM((NPEER, NZ, 8, LANES), F32),
            pltpu.VMEM((HALF, LANES), jnp.int32),
            pltpu.VMEM((RUN + 1, NPEER, LANES), jnp.int32),
            pltpu.VMEM((HALF, 2 * rows2, width), BF16),
            pltpu.VMEM((HALF, NPEER, 2 * KINDS, width), BF16),
            pltpu.VMEM((NPEER, HALF, 2 * KINDS, width), BF16),
            pltpu.VMEM((NY, NPEER, 8, rows2), F32),
            pltpu.VMEM((NZ, 1, rows2), F32),
            pltpu.VMEM((NPEER, NZ, 1, rows2), F32),
            pltpu.VMEM((2, NY, rows, width), BF16),
            pltpu.VMEM((2, NY - 1, rows, width), BF16),
            pltpu.VMEM((rows, width), F32),
        ]
        + both(NY - 1)
        + both(2, HALF)
        + both(NPEER - 1)
        + both(2, HALF, APARTS)
        + both(2, HALF)
        + both(NX - 1)
        + both(2, NZ)
        + both(2, NZ)
        + both(2, NZ)
        + both(2, HALF, EPARTS)
        + both(HALF, NPEER - 1)
        + both(NY - 1)
        + both(NZ - 1)
        + both(NPEER - 1)
        + both(2, NY - 1),
        compiler_params=pltpu.CompilerParams(
            collective_id=0, has_side_effects=True, vmem_limit_bytes=56 * 1024 * 1024
        ),
        cost_estimate=pl.CostEstimate(
            flops=3 * 10**9, bytes_accessed=10**8, transcendentals=10**5
        ),
        name="contrastive_backward",
    )(q_hidden, p_hidden, proj, negatives.T, positives[None, :])
    return (grad_q, grad_p, loss[0])


def solution(mesh):
    placed = (P("dp", "mp"), P("dp", "mp"), P("dp", "mp"), P("dp"), P("dp", None))
    return jax.shard_map(
        body,
        mesh=mesh,
        in_specs=placed,
        out_specs=(P("dp", "mp"), P("dp", "mp"), P("dp")),
        check_vma=False,
    )
```

```python
import functools

import jax
import jax.numpy as jnp
from jax import lax
from jax.experimental import pallas as pl
from jax.experimental.pallas import tpu as pltpu
from jax.sharding import PartitionSpec as P

SCALE = 20.0
EPS = 1e-06
MESH = pl.DeviceIdType.MESH
F32 = jnp.float32
BF16 = jnp.bfloat16

NX, NZ, NC, NY = 4, 16, 2, 4
NDP = NX * NZ * NC
NPEER = NX * NC
HALF = NZ // 2
RUN = 4
CAP = 3
LANES = 128
XFIRST = 384
APARTS = 4
EPARTS = 4
KINDS = 8


def coords():
    dp = lax.axis_index("dp")
    y = lax.axis_index("mp")
    core = lax.rem(dp, NC)
    chip = lax.div(dp, NC)
    return lax.div(chip, NZ), y, lax.rem(chip, NZ), core


def dp_index(x, z, core):
    return (x * NZ + z) * NC + core


def wrap(value, size):
    return lax.rem(value + 2 * size, size)


def remote(src, dst, send_sem, recv_sem, dp, y):
    return pltpu.make_async_remote_copy(
        src_ref=src,
        dst_ref=dst,
        send_sem=send_sem,
        recv_sem=recv_sem,
        device_id=(dp, y),
        device_id_type=MESH,
    )


def nt(a, b):
    return lax.dot_general(a, b, (((1,), (1,)), ((), ())), preferred_element_type=F32)


def mm(a, b):
    return jnp.dot(a, b, preferred_element_type=F32)


def onehot(mask):
    return jnp.where(mask, 1.0, 0.0).astype(BF16)


def iota(shape, dim):
    return lax.broadcasted_iota(jnp.int32, shape, dim)


def down(mask, value):
    return jnp.sum(jnp.where(mask, value, 0.0), axis=0, keepdims=True)


def across(mask, value):
    return jnp.sum(jnp.where(mask, value, 0.0), axis=1, keepdims=True)


def greet(peers):
    barrier = pltpu.get_barrier_semaphore()
    for dp, y in peers:
        pl.semaphore_signal(barrier, inc=1, device_id=(dp, y), device_id_type=MESH)
    pl.semaphore_wait(barrier, len(peers))


def run_table(neg_ref, rows):
    holder = iota((rows, LANES), 1)
    query = iota((rows, LANES), 0).astype(F32)
    holder = dp_index(
        lax.div(holder, NZ * NC), lax.rem(holder, NZ), lax.rem(lax.div(holder, NZ), NC)
    ).astype(F32)
    before = onehot(iota((rows, rows), 1) < iota((rows, rows), 0))
    base = jnp.zeros((1, LANES), F32)
    passages = [base] * RUN
    queries = [base] * CAP
    ids = neg_ref[...]
    turn = onehot(iota((rows, rows), 0) == iota((rows, rows), 1))
    owners = nt(turn, lax.div(ids, rows).astype(F32).astype(BF16))
    locals_ = nt(turn, lax.rem(ids, rows).astype(F32).astype(BF16))
    for r in range(neg_ref.shape[0] // RUN):
        hit = owners[:, RUN * r : RUN * r + 1] == holder
        rank = mm(before, onehot(hit)) + base
        base = base + jnp.sum(jnp.where(hit, 1.0, 0.0), axis=0, keepdims=True)
        for i in range(CAP):
            queries[i] = queries[i] + down(hit & (rank == float(i)), query + 1.0)
        for j in range(RUN):
            local = locals_[:, RUN * r + j : RUN * r + j + 1]
            named = jnp.max(jnp.where(hit, local, 0.0), axis=0, keepdims=True)
            passages[j] = jnp.maximum(passages[j], named)
    return jnp.concatenate(passages + [q - 1.0 for q in queries] + [jnp.full((1, LANES), -1.0)], 0)


def seen_z(z, step, second):
    ahead = jnp.where(step == 0, HALF, step)
    return lax.rem(jnp.where(second == 0, z - step + NZ, z + ahead), NZ)


def fill_picks(tab, sel_ref, rank, z, rows):
    lane8 = iota((NPEER, LANES), 1)
    row8 = iota((NPEER, LANES), 0)
    row = iota((LANES, LANES), 0)
    lane = iota((LANES, LANES), 1)
    kind = lax.rem(lane8, KINDS)
    second = lax.rem(lax.div(lane8, KINDS), 2)
    kind_l = lax.rem(lane, KINDS)
    second_l = lax.rem(lax.div(lane, KINDS), 2)
    group_l = lax.div(lane, 2 * KINDS)
    asked = jnp.concatenate([tab[d, z] for d in range(NPEER) for _ in range(2)], axis=0).astype(BF16)
    zero8 = jnp.zeros_like(row8)
    firsts = nt(onehot(lane8 == rank * NZ + seen_z(z, row8, zero8)), asked)
    seconds = nt(onehot(lane8 == rank * NZ + seen_z(z, row8, zero8 + 1)), asked)
    from_p = jnp.where(second == 0, firsts, seconds) + float(rows)
    here = tab[rank].reshape(LANES, LANES).astype(BF16)
    spread = mm(here, onehot(row == group_l * NZ + z))
    from_q = jnp.concatenate(
        [
            down(row == seen_z(z, jnp.full_like(lane, s), second_l) * KINDS + kind_l, spread)
            for s in range(HALF)
        ],
        axis=0,
    )
    picked = jnp.where(kind < RUN, from_p, from_q)
    picked = jnp.where(picked >= 0.0, picked + (second * 2 * rows).astype(F32), -1.0)
    sel_ref[...] = picked.astype(jnp.int32)


def about_this(tab, rank, z):
    lane8 = iota((NPEER, LANES), 1)
    row = iota((LANES, LANES), 0)
    lane = iota((LANES, LANES), 1)
    me_row = onehot(lane8 == rank * NZ + z)
    said = [nt(me_row, tab[d].reshape(LANES, LANES).astype(BF16))[0:1] for d in range(NPEER)]
    said = jnp.concatenate(said, axis=0)
    low = said.astype(BF16)
    first = lane - lax.rem(lane, KINDS)
    passages = [mm(low, onehot(row == first + r)) for r in range(RUN)]
    return jnp.concatenate([said] + passages, axis=0).astype(BF16)


def fill_meets(tab, about, idx_ref, step, rank, z, rows):
    row = iota((LANES, LANES), 0)
    lane = iota((LANES, LANES), 1)
    kind_l = lax.rem(lane, KINDS)
    group_l = lax.div(lane, 2 * KINDS)
    z_l = seen_z(z, jnp.full_like(lane, step), lax.rem(lax.div(lane, KINDS), 2))
    kind = kind_l[0:1]
    own = mm(tab[rank, z].astype(BF16), onehot(row == group_l * NZ + z_l))
    found = mm(about, onehot(row == z_l * KINDS + kind_l))
    from_peer = row[0:NPEER] == group_l[0:NPEER]
    picked = [down(from_peer, found[NPEER * k : NPEER * (k + 1)]) for k in range(RUN + 1)]
    wants = picked[0]
    out = []
    for r in range(RUN):
        theirs = jnp.where(wants >= 0.0, picked[1 + r] + float(rows), -1.0)
        out.append(jnp.where(kind < RUN, own[RUN + r : RUN + r + 1], theirs))
    out.append(jnp.where(kind < RUN, -1.0, wants))
    out += [jnp.full((1, LANES), -1.0)] * (8 - len(out))
    idx_ref[step] = jnp.concatenate(out, axis=0).astype(jnp.int32)


def fused_kernel(
    hq_ref,
    hp_ref,
    w_ref,
    neg_ref,
    pos_ref,
    gq_ref,
    gp_ref,
    loss_ref,
    hid,
    wbuf,
    tab,
    sel_ref,
    idx_ref,
    col,
    outbox,
    recv,
    ybuf,
    dz,
    dtab,
    gpart,
    gin,
    acc,
    h_s,
    h_r,
    t_s,
    t_r,
    u_s,
    u_r,
    a_s,
    a_r,
    b_s,
    b_r,
    ax_s,
    ax_r,
    bx_s,
    bx_r,
    bd_s,
    bd_r,
    c_s,
    c_r,
    z_s,
    z_r,
    p_s,
    p_r,
    y_s,
    y_r,
    d_s,
    d_r,
    e_s,
    e_r,
    g_s,
    g_r,
):
    x, y, z, core = coords()
    me = dp_index(x, z, core)
    rank = x * NC + core
    rows, width = hq_ref.shape
    rows2 = 2 * rows
    depth = w_ref.shape[0]
    right = dp_index(x, wrap(z + 1, NZ), core)
    left = dp_index(x, wrap(z - 1, NZ), core)
    x_next = dp_index(wrap(x + 1, NX), z, core)
    x_prev = dp_index(wrap(x - 1, NX), z, core)
    sibling = dp_index(x, z, 1 - core)

    def peer_of(k):
        other = wrap(rank + k, NPEER)
        return dp_index(lax.div(other, NC), z, lax.rem(other, NC))

    y_peers = [wrap(y + k, NY) for k in range(1, NY)]
    z_peers = [dp_index(x, wrap(z + k, NZ), core) for k in range(1, NZ)]
    mates = [peer_of(k) for k in range(1, NPEER)]
    greet([(me, p) for p in y_peers] + [(right, y), (left, y)] + [(p, y) for p in mates])

    def send(src, dst, send_sem, recv_sem, dp, at_y):
        cp = remote(src, dst, send_sem, recv_sem, dp, at_y)
        cp.start()
        return cp

    def drain(ref, sem):
        pltpu.make_async_copy(ref, ref, sem).wait()

    def base_of(zb):
        return pl.multiple_of((zb * NC + core) * depth, depth)

    first_cols = pl.ds(0, XFIRST)
    other_cols = pl.ds(XFIRST, width - XFIRST)

    def a_block(zb, lo, count):
        return wbuf.at[pl.ds(lo, count), pl.ds(base_of(zb), depth), first_cols]

    def b_block(xb, zb, lo=0, count=depth):
        return wbuf.at[xb, pl.ds(pl.multiple_of(base_of(zb) + lo, count), count), other_cols]

    def z_of(block):
        if block <= HALF:
            return wrap(z - block, NZ)
        return wrap(z + block - HALF, NZ)

    def a_ring(direction, step, piece):
        zb = wrap(z - (step - 1), NZ) if direction == 0 else wrap(z + (step - 1), NZ)
        part = a_block(zb, piece * (NX // APARTS), NX // APARTS)
        to = right if direction == 0 else left
        at = (direction, step - 1, piece)
        return send(part, part, a_s, a_r.at[at], to, y)

    def t_ring(direction, step):
        zb = wrap(z - (step - 1), NZ) if direction == 0 else wrap(z + (step - 1), NZ)
        part = tab.at[rank, zb]
        to = right if direction == 0 else left
        return send(part, part, t_s, t_r.at[direction, step - 1], to, y)

    def b_ring(direction, step):
        zb = wrap(z - (step - 1), NZ) if direction == 0 else wrap(z + (step - 1), NZ)
        if step < HALF:
            part = b_block(x, zb)
        else:
            part = b_block(x, zb, direction * (depth // 2), depth // 2)
        to = right if direction == 0 else left
        return send(part, part, b_s, b_r.at[direction, step - 1], to, y)

    def b_over_x(block):
        part = b_block(x, z_of(block))
        return [
            send(part, part, bx_s, bx_r.at[way, block], to, y)
            for way, to in ((0, x_next), (1, x_prev))
        ]

    def b_across(block, copies):
        for way, to in ((0, x_next), (1, x_prev)):
            copies[way].wait_recv()
            xb = wrap(x - 1, NX) if way == 0 else wrap(x + 1, NX)
            part = b_block(xb, z_of(block), way * (depth // 2), depth // 2)
            send(part, part, bd_s, bd_r.at[block], to, y)

    def to_sibling(cols, block):
        part = wbuf.at[:, pl.ds(base_of(z_of(block)), depth), cols]
        send(part, part, c_s, c_r, sibling, y)

    wbuf[x, pl.ds(base_of(z), depth), :] = w_ref[...]
    own_first = wbuf.at[x, pl.ds(base_of(z), depth), first_cols]
    for k in range(1, NX):
        send(own_first, own_first, ax_s, ax_r, dp_index(wrap(x + k, NX), z, core), y)
    b_live = {(way, 1): b_ring(way, 1) for way in range(2)}
    over_x = {0: b_over_x(0)}
    hid[y, 0:rows, :] = hq_ref[...]
    hid[y, rows:rows2, :] = hp_ref[...]
    for peer in y_peers:
        send(hid.at[y], hid.at[y], h_s, h_r, me, peer)
    drain(wbuf.at[0, pl.ds(0, (NX - 1) * depth), first_cols], ax_r)
    a_live = {}
    for piece in range(APARTS):
        for way in range(2):
            a_live[way, 1, piece] = a_ring(way, 1, piece)
    to_sibling(first_cols, 0)

    tab[rank, z] = run_table(neg_ref, rows)
    t_live = {(way, 1): t_ring(way, 1) for way in range(2)}

    blocks_of = {0: [0]}
    for step in range(1, HALF):
        blocks_of[step] = [step, HALF + step]
    blocks_of[HALF] = [HALF]

    def finish(step):
        for block in blocks_of[step]:
            drain(b_block(x, z), bd_r.at[block])
            to_sibling(other_cols, block)

    def turn(step):
        for block in blocks_of[step]:
            b_across(block, over_x[block])

    for turn_at in range(1, HALF + 2):
        step = turn_at
        if step <= HALF:
            for way in range(2):
                b_live[way, step].wait_recv()
                if step < HALF:
                    b_live[way, step + 1] = b_ring(way, step + 1)
                    over_x[blocks_of[step][way]] = b_over_x(blocks_of[step][way])
            if step == HALF:
                over_x[HALF] = b_over_x(HALF)
        step = turn_at - 1
        if step >= 1:
            for piece in range(APARTS):
                for way in range(2):
                    if (way, step, piece) not in a_live:
                        continue
                    a_live[way, step, piece].wait_recv()
                    if step + 1 < HALF or (step + 1 == HALF and piece * 2 // APARTS == way):
                        a_live[way, step + 1, piece] = a_ring(way, step + 1, piece)
            for way in range(2):
                if (way, step) in t_live:
                    t_live[way, step].wait_recv()
                    if step + 1 < HALF or (step + 1 == HALF and way == 0):
                        t_live[way, step + 1] = t_ring(way, step + 1)
            for block in blocks_of[step]:
                to_sibling(first_cols, block)
        if turn_at >= 2:
            turn(turn_at - 2)
        if turn_at >= 4:
            finish(turn_at - 4)
    for k, peer in enumerate(mates):
        send(tab.at[rank], tab.at[rank], u_s, u_r, peer, y)
    turn(HALF)
    for step in range(HALF - 2, HALF + 1):
        finish(step)
    drain(wbuf.at[:, pl.ds(0, NZ * depth)], c_r)
    drain(hid.at[pl.ds(0, NY - 1)], h_r)

    tile = width // EPARTS

    def ring(direction, step, piece):
        src_at = 0 if direction == 0 or step == 1 else rows2
        cols = pl.ds(piece * tile, tile)
        src = col.at[step - 1, pl.ds(src_at, rows2), cols]
        if step < HALF:
            dst = col.at[step, pl.ds(direction * rows2, rows2), cols]
        else:
            dst = col.at[0, pl.ds(rows2, rows2), cols]
        to = right if direction == 0 else left
        at = (direction, step - 1, piece)
        return send(src, dst, z_s, z_r.at[at], to, y)

    live = {}
    for piece in range(EPARTS):
        total = jnp.zeros((rows2, tile), F32)
        for b in range(NY):
            total = total + mm(hid[b], wbuf[b, :, piece * tile : (piece + 1) * tile])
        col[0, 0:rows2, piece * tile : (piece + 1) * tile] = total.astype(BF16)
        for direction in range(2):
            live[direction, 1, piece] = ring(direction, 1, piece)
    drain(tab.at[pl.ds(0, NPEER - 1)], u_r)
    fill_picks(tab, sel_ref, rank, z, rows)
    about = about_this(tab, rank, z)

    lane = iota((1, rows2), 1)
    row_id = iota((rows2, rows2), 0)
    lane_id = iota((rows2, rows2), 1)
    eye = row_id == lane_id
    emb = col[0, 0:rows2, :]
    local = lax.rem(pos_ref[...], rows)
    partner = jnp.concatenate([local, local], axis=1).astype(F32)
    partner_col = across(eye, partner).astype(jnp.int32)
    partner = partner.astype(jnp.int32)
    pair = ((lane_id < rows) & (row_id == partner + rows)) | (
        (row_id < rows) & (lane_id == partner_col + rows)
    )
    gram = nt(emb, emb)
    own_sq = down(eye, gram)
    own_pos = down(pair, gram)

    def mask_of(s, r):
        return row_id == idx_ref[s, r : r + 1, :]

    def score(s):
        fill_meets(tab, about, idx_ref, s, rank, z, rows)
        drain(recv.at[s, pl.ds(0, NPEER - 1)], p_r.at[s])
        got = recv[s].reshape(rows2, width)
        cross = nt(emb, got)
        parts = [down(mask_of(s, r), cross) for r in range(RUN)]
        parts += [down(eye, nt(got, got)), own_sq, own_pos, jnp.zeros_like(own_sq)]
        ybuf[y, s] = jnp.concatenate(parts, axis=0)

    pair_rows = iota((2 * rows2, LANES), 0)
    for step in range(1, HALF + 1):
        for piece in range(EPARTS):
            for direction in range(2):
                if (direction, step, piece) not in live:
                    continue
                live[direction, step, piece].wait_recv()
                if step + 1 < HALF or (step + 1 == HALF and piece * 2 // EPARTS == direction):
                    live[direction, step + 1, piece] = ring(direction, step + 1, piece)
        slot = step % HALF
        pick = onehot(pair_rows == sel_ref[slot : slot + 1, :])
        picked = lax.dot_general(
            pick, col[slot], (((0,), (0,)), ((), ())), preferred_element_type=F32
        )
        outbox[slot] = picked.astype(BF16).reshape(NPEER, 2 * KINDS, width)
        for k, peer in enumerate(mates):
            src = outbox.at[slot, wrap(rank + k + 1, NPEER)]
            send(src, recv.at[slot, rank], p_s, p_r.at[slot], peer, y)
        recv[slot, rank] = outbox[slot, rank]
        if step > 1:
            score(step - 1)
    score(0)

    for peer in y_peers:
        send(ybuf.at[y], ybuf.at[y], y_s, y_r, me, peer)
    drain(ybuf.at[pl.ds(0, NY - 1)], y_r)

    sums = [((ybuf[0, s] + ybuf[1, s]) + ybuf[2, s]) + ybuf[3, s] for s in range(HALF)]
    inv_row = 1.0 / jnp.sqrt(sums[0][5:6] + EPS)
    inv_col = across(eye, inv_row)
    pos_score = SCALE * sums[0][6:7] * inv_row * down(pair, inv_col)
    pos_exp = jnp.exp(pos_score)
    denom = across(eye, pos_exp)
    scores = []
    exps = []
    lane_inv = []
    for d in range(HALF):
        rl = 1.0 / jnp.sqrt(sums[d][4:5] + EPS)
        lane_inv.append(rl)
        sc = []
        ex = []
        for r in range(RUN):
            mask = mask_of(d, r)
            s = SCALE * sums[d][r : r + 1] * rl * down(mask, inv_col)
            e = jnp.exp(s)
            sc.append(s)
            ex.append(e)
            denom = denom + across(mask, e)
        scores.append(sc)
        exps.append(ex)
    denom_row = down(eye, denom)
    loss_ref[...] = jnp.log(denom_row[:, 0:rows]) - pos_score[:, 0:rows]
    is_query = lane < rows
    dinv_row = jnp.where(is_query, 1.0 / denom_row, 0.0)
    dinv_col = across(eye, dinv_row)

    dz[0] = dinv_row
    for k, peer in enumerate(z_peers):
        send(dz.at[0], dz.at[k + 1], d_s, d_r, peer, y)

    pos_coef = jnp.where(is_query, SCALE * (pos_exp * dinv_row - 1.0), 0.0)
    pos_coef = pos_coef + down(pair, across(eye, pos_coef))

    def half(part):
        return slice(part * rows, (part + 1) * rows)

    def half_weights(part, dinv_at):
        half_id = iota((rows, rows2), 0) + part * rows
        weights = []
        inners = []
        for s in range(HALF):
            weight = jnp.zeros((rows, rows2), F32)
            inner = jnp.zeros((rows, rows2), F32)
            for r in range(RUN):
                mask = half_id == idx_ref[s, r : r + 1, :]
                coef = exps[s][r] * dinv_at(s, r)
                weight = weight + jnp.where(mask, SCALE * coef * lane_inv[s], 0.0)
                inner = inner + jnp.where(mask, coef * scores[s][r], 0.0)
            weights.append(weight)
            inners.append(inner)
        return weights, inners

    def half_grads(part, weights, inner):
        def add_rows(weight, values, fresh=False):
            high = weight.astype(BF16)
            low = (weight - high.astype(F32)).astype(BF16)
            term = mm(jnp.concatenate([high, low], axis=0), values)
            term = term[0:rows] + term[rows:]
            acc[...] = term if fresh else acc[...] + term

        half_pair = pair[half(part)]
        add_rows(jnp.where(half_pair, pos_coef * inv_row, 0.0), emb, True)
        inner = jnp.sum(inner, axis=1, keepdims=True)
        inner = inner + across(half_pair, pos_coef * pos_score * (1.0 / SCALE))
        for s in range(HALF):
            add_rows(weights[s], recv[s].reshape(rows2, width))
        unit = emb[half(part)].astype(F32) * inv_col[half(part)]
        return ((acc[...] - unit * inner) * inv_col[half(part)]).astype(BF16)

    def project(part, g_emb):
        for k in (2, 1, 3, NY):
            block = wrap(y + k, NY)
            gpart[part, k - 1] = nt(g_emb, wbuf[block]).astype(BF16)
            if k < NY:
                mine = gpart.at[part, k - 1]
                theirs = gin.at[part, k - 1]
                send(mine, theirs, g_s, g_r.at[part], me, block)

    def gathered(part):
        total = gpart[part, NY - 1].astype(F32)
        drain(gin.at[part], g_r.at[part])
        for k in range(NY - 1):
            total = total + gin[part, k].astype(F32)
        return total.astype(BF16)

    weights, inners = half_weights(0, lambda s, r: down(mask_of(s, r), dinv_col))
    g_query = half_grads(0, weights, sum(inners))
    drain(dz.at[pl.ds(0, NZ - 1)], d_r)
    for k, peer in enumerate(mates):
        send(dz, dtab.at[k + 1], e_s, e_r, peer, y)
    for k in range(NZ):
        dtab[0, k] = dz[k]
    project(0, g_query)

    weights, inners = half_weights(1, lambda s, r: 1.0)
    drain(dtab.at[pl.ds(0, NPEER - 1)], e_r)
    at_source = iota((NZ, rows2), 0) == lax.div(iota((NZ, rows2), 1), KINDS)
    inner = jnp.zeros((rows, rows2), F32)
    for s in range(HALF):
        ahead = (s, NZ - s) if s else (0, HALF)
        table = [dtab[wrap(rank - d, NPEER), k] for d in range(NPEER) for k in ahead]
        table = jnp.concatenate(table, axis=0)
        spread = jnp.where(row_id == idx_ref[s, RUN : RUN + 1, :], 1.0, 0.0)
        found = jnp.dot(table, spread, preferred_element_type=F32, precision=lax.Precision.HIGHEST)
        their_inv = down(at_source, found)
        weights[s] = weights[s] * their_inv
        inner = inner + inners[s] * their_inv
    project(1, half_grads(1, weights, inner))
    gq_ref[...] = gathered(0)
    gp_ref[...] = gathered(1)

    drain(hid.at[pl.ds(0, NY - 1)], h_s)
    drain(tab.at[0, pl.ds(0, NZ - 1)], t_s)
    drain(tab.at[pl.ds(0, NPEER - 1)], u_s)
    drain(wbuf.at[:, pl.ds(0, (NZ - 1) * depth), first_cols], a_s)
    drain(wbuf.at[0, pl.ds(0, (NZ - 1) * depth), other_cols], b_s)
    drain(wbuf.at[0, pl.ds(0, (NX - 1) * depth), first_cols], ax_s)
    drain(wbuf.at[0, pl.ds(0, 2 * NZ * depth), other_cols], bx_s)
    drain(wbuf.at[0, pl.ds(0, NZ * depth), other_cols], bd_s)
    drain(wbuf.at[:, pl.ds(0, NZ * depth)], c_s)
    drain(col.at[:, pl.ds(0, rows2 * (NZ - 1) // HALF)], z_s)
    drain(outbox.at[:, pl.ds(0, NPEER - 1)], p_s)
    drain(ybuf.at[pl.ds(0, NY - 1)], y_s)
    drain(dz.at[pl.ds(0, NZ - 1)], d_s)
    drain(dtab.at[pl.ds(0, NPEER - 1)], e_s)
    drain(gin, g_s)


def body(q_hidden, p_hidden, proj, positives, negatives):
    rows, width = q_hidden.shape
    rows2 = 2 * rows
    block = proj.shape[0] * NDP // NX
    vmem = pl.BlockSpec(memory_space=pltpu.VMEM)
    dma = pltpu.SemaphoreType.DMA

    grad_q, grad_p, loss = pl.pallas_call(
        fused_kernel,
        out_shape=(
            jax.ShapeDtypeStruct((rows, width), BF16),
            jax.ShapeDtypeStruct((rows, width), BF16),
            jax.ShapeDtypeStruct((1, rows), F32),
        ),
        in_specs=[vmem] * 5,
        out_specs=(vmem,) * 3,
        scratch_shapes=[
            pltpu.VMEM((NY, rows2, width), BF16),
            pltpu.VMEM((NX, block, width), BF16),
            pltpu.VMEM((NPEER, NZ, 8, LANES), F32),
            pltpu.VMEM((HALF, LANES), jnp.int32),
            pltpu.VMEM((HALF, 8, LANES), jnp.int32),
            pltpu.VMEM((HALF, 2 * rows2, width), BF16),
            pltpu.VMEM((HALF, NPEER, 2 * KINDS, width), BF16),
            pltpu.VMEM((HALF, NPEER, 2 * KINDS, width), BF16),
            pltpu.VMEM((NY, NPEER, 8, rows2), F32),
            pltpu.VMEM((NZ, 1, rows2), F32),
            pltpu.VMEM((NPEER, NZ, 1, rows2), F32),
            pltpu.VMEM((2, NY, rows, width), BF16),
            pltpu.VMEM((2, NY - 1, rows, width), BF16),
            pltpu.VMEM((rows, width), F32),
        ]
        + [dma, dma]
        + [dma, dma((2, HALF))]
        + [dma, dma]
        + [dma, dma((2, HALF, APARTS))]
        + [dma, dma((2, HALF))]
        + [dma, dma]
        + [dma, dma((2, NZ))]
        + [dma, dma((NZ,))]
        + [dma, dma]
        + [dma, dma((2, HALF, EPARTS))]
        + [dma, dma((HALF,))]
        + [dma, dma]
        + [dma, dma]
        + [dma, dma]
        + [dma, dma((2,))],
        compiler_params=pltpu.CompilerParams(
            collective_id=0, has_side_effects=True, vmem_limit_bytes=56 * 1024 * 1024
        ),
        cost_estimate=pl.CostEstimate(
            flops=3 * 10**9, bytes_accessed=10**8, transcendentals=10**5
        ),
        name="contrastive_backward",
    )(q_hidden, p_hidden, proj, negatives.T, positives[None, :])
    return (grad_q, grad_p, loss[0])


def solution(mesh):
    placed = (P("dp", "mp"), P("dp", "mp"), P("dp", "mp"), P("dp"), P("dp", None))
    return jax.shard_map(
        body,
        mesh=mesh,
        in_specs=placed,
        out_specs=(P("dp", "mp"), P("dp", "mp"), P("dp")),
        check_vma=False,
    )
```

```python
import functools

import jax
import jax.numpy as jnp
from jax import lax
from jax.experimental import pallas as pl
from jax.experimental.pallas import tpu as pltpu
from jax.sharding import PartitionSpec as P

SCALE = 20.0
EPS = 1e-06
MESH = pl.DeviceIdType.MESH
F32 = jnp.float32
BF16 = jnp.bfloat16

NX, NZ, NC, NY = 4, 16, 2, 4
NDP = NX * NZ * NC
NPEER = NX * NC
HALF = NZ // 2
RUN = 4
CAP = 3
LANES = 128
XFIRST = 256
APARTS = 4
EPARTS = 4
KINDS = 8


def coords():
    dp = lax.axis_index("dp")
    y = lax.axis_index("mp")
    core = lax.rem(dp, NC)
    chip = lax.div(dp, NC)
    return lax.div(chip, NZ), y, lax.rem(chip, NZ), core


def dp_index(x, z, core):
    return (x * NZ + z) * NC + core


def wrap(value, size):
    return lax.rem(value + 2 * size, size)


def remote(src, dst, send_sem, recv_sem, dp, y):
    return pltpu.make_async_remote_copy(
        src_ref=src,
        dst_ref=dst,
        send_sem=send_sem,
        recv_sem=recv_sem,
        device_id=(dp, y),
        device_id_type=MESH,
    )


def nt(a, b):
    return lax.dot_general(a, b, (((1,), (1,)), ((), ())), preferred_element_type=F32)


def mm(a, b):
    return jnp.dot(a, b, preferred_element_type=F32)


def onehot(mask):
    return jnp.where(mask, 1.0, 0.0).astype(BF16)


def iota(shape, dim):
    return lax.broadcasted_iota(jnp.int32, shape, dim)


def down(mask, value):
    return jnp.sum(jnp.where(mask, value, 0.0), axis=0, keepdims=True)


def across(mask, value):
    return jnp.sum(jnp.where(mask, value, 0.0), axis=1, keepdims=True)


def greet(peers):
    barrier = pltpu.get_barrier_semaphore()
    for dp, y in peers:
        pl.semaphore_signal(barrier, inc=1, device_id=(dp, y), device_id_type=MESH)
    pl.semaphore_wait(barrier, len(peers))


def run_table(neg_ref, rows):
    holder = iota((rows, LANES), 1)
    query = iota((rows, LANES), 0).astype(F32)
    holder = dp_index(
        lax.div(holder, NZ * NC), lax.rem(holder, NZ), lax.rem(lax.div(holder, NZ), NC)
    ).astype(F32)
    before = onehot(iota((rows, rows), 1) < iota((rows, rows), 0))
    base = jnp.zeros((1, LANES), F32)
    passages = [base] * RUN
    queries = [base] * CAP
    ids = neg_ref[...]
    turn = onehot(iota((rows, rows), 0) == iota((rows, rows), 1))
    owners = nt(turn, lax.div(ids, rows).astype(F32).astype(BF16))
    locals_ = nt(turn, lax.rem(ids, rows).astype(F32).astype(BF16))
    for r in range(neg_ref.shape[0] // RUN):
        hit = owners[:, RUN * r : RUN * r + 1] == holder
        rank = mm(before, onehot(hit)) + base
        base = base + jnp.sum(jnp.where(hit, 1.0, 0.0), axis=0, keepdims=True)
        for i in range(CAP):
            queries[i] = queries[i] + down(hit & (rank == float(i)), query + 1.0)
        for j in range(RUN):
            local = locals_[:, RUN * r + j : RUN * r + j + 1]
            named = jnp.max(jnp.where(hit, local, 0.0), axis=0, keepdims=True)
            passages[j] = jnp.maximum(passages[j], named)
    return jnp.concatenate(passages + [q - 1.0 for q in queries] + [jnp.full((1, LANES), -1.0)], 0)


def seen_z(z, step, second):
    ahead = jnp.where(step == 0, HALF, step)
    return lax.rem(jnp.where(second == 0, z - step + NZ, z + ahead), NZ)


def fill_picks(tab, sel_ref, rank, z, rows):
    lane8 = iota((NPEER, LANES), 1)
    row8 = iota((NPEER, LANES), 0)
    row = iota((LANES, LANES), 0)
    lane = iota((LANES, LANES), 1)
    kind = lax.rem(lane8, KINDS)
    second = lax.rem(lax.div(lane8, KINDS), 2)
    kind_l = lax.rem(lane, KINDS)
    second_l = lax.rem(lax.div(lane, KINDS), 2)
    group_l = lax.div(lane, 2 * KINDS)
    asked = jnp.concatenate([tab[d, z] for d in range(NPEER) for _ in range(2)], axis=0).astype(BF16)
    zero8 = jnp.zeros_like(row8)
    firsts = nt(onehot(lane8 == rank * NZ + seen_z(z, row8, zero8)), asked)
    seconds = nt(onehot(lane8 == rank * NZ + seen_z(z, row8, zero8 + 1)), asked)
    from_p = jnp.where(second == 0, firsts, seconds) + float(rows)
    here = tab[rank].reshape(LANES, LANES).astype(BF16)
    spread = mm(here, onehot(row == group_l * NZ + z))
    from_q = jnp.concatenate(
        [
            down(row == seen_z(z, jnp.full_like(lane, s), second_l) * KINDS + kind_l, spread)
            for s in range(HALF)
        ],
        axis=0,
    )
    picked = jnp.where(kind < RUN, from_p, from_q)
    picked = jnp.where(picked >= 0.0, picked + (second * 2 * rows).astype(F32), -1.0)
    sel_ref[...] = picked.astype(jnp.int32)


def about_this(tab, rank, z):
    lane8 = iota((NPEER, LANES), 1)
    row = iota((LANES, LANES), 0)
    lane = iota((LANES, LANES), 1)
    me_row = onehot(lane8 == rank * NZ + z)
    said = [nt(me_row, tab[d].reshape(LANES, LANES).astype(BF16))[0:1] for d in range(NPEER)]
    said = jnp.concatenate(said, axis=0)
    low = said.astype(BF16)
    first = lane - lax.rem(lane, KINDS)
    passages = [mm(low, onehot(row == first + r)) for r in range(RUN)]
    return jnp.concatenate([said] + passages, axis=0).astype(BF16)


def fill_meets(tab, about, idx_ref, step, rank, z, rows):
    row = iota((LANES, LANES), 0)
    lane = iota((LANES, LANES), 1)
    kind_l = lax.rem(lane, KINDS)
    group_l = lax.div(lane, 2 * KINDS)
    z_l = seen_z(z, jnp.full_like(lane, step), lax.rem(lax.div(lane, KINDS), 2))
    kind = kind_l[0:1]
    own = mm(tab[rank, z].astype(BF16), onehot(row == group_l * NZ + z_l))
    found = mm(about, onehot(row == z_l * KINDS + kind_l))
    from_peer = row[0:NPEER] == group_l[0:NPEER]
    picked = [down(from_peer, found[NPEER * k : NPEER * (k + 1)]) for k in range(RUN + 1)]
    wants = picked[0]
    out = []
    for r in range(RUN):
        theirs = jnp.where(wants >= 0.0, picked[1 + r] + float(rows), -1.0)
        out.append(jnp.where(kind < RUN, own[RUN + r : RUN + r + 1], theirs))
    out.append(jnp.where(kind < RUN, -1.0, wants))
    out += [jnp.full((1, LANES), -1.0)] * (8 - len(out))
    idx_ref[step] = jnp.concatenate(out, axis=0).astype(jnp.int32)


def fused_kernel(
    hq_ref,
    hp_ref,
    w_ref,
    neg_ref,
    pos_ref,
    gq_ref,
    gp_ref,
    loss_ref,
    hid,
    wbuf,
    tab,
    sel_ref,
    idx_ref,
    col,
    outbox,
    recv,
    ybuf,
    dz,
    dtab,
    gpart,
    gin,
    acc,
    h_s,
    h_r,
    t_s,
    t_r,
    u_s,
    u_r,
    a_s,
    a_r,
    b_s,
    b_r,
    ax_s,
    ax_r,
    bx_s,
    bx_r,
    bd_s,
    bd_r,
    c_s,
    c_r,
    z_s,
    z_r,
    p_s,
    p_r,
    y_s,
    y_r,
    d_s,
    d_r,
    e_s,
    e_r,
    g_s,
    g_r,
):
    x, y, z, core = coords()
    me = dp_index(x, z, core)
    rank = x * NC + core
    rows, width = hq_ref.shape
    rows2 = 2 * rows
    depth = w_ref.shape[0]
    right = dp_index(x, wrap(z + 1, NZ), core)
    left = dp_index(x, wrap(z - 1, NZ), core)
    x_next = dp_index(wrap(x + 1, NX), z, core)
    x_prev = dp_index(wrap(x - 1, NX), z, core)
    sibling = dp_index(x, z, 1 - core)

    def peer_of(k):
        other = wrap(rank + k, NPEER)
        return dp_index(lax.div(other, NC), z, lax.rem(other, NC))

    y_peers = [wrap(y + k, NY) for k in range(1, NY)]
    z_peers = [dp_index(x, wrap(z + k, NZ), core) for k in range(1, NZ)]
    mates = [peer_of(k) for k in range(1, NPEER)]
    greet([(me, p) for p in y_peers] + [(right, y), (left, y)] + [(p, y) for p in mates])

    def send(src, dst, send_sem, recv_sem, dp, at_y):
        cp = remote(src, dst, send_sem, recv_sem, dp, at_y)
        cp.start()
        return cp

    def drain(ref, sem):
        pltpu.make_async_copy(ref, ref, sem).wait()

    def base_of(zb):
        return pl.multiple_of((zb * NC + core) * depth, depth)

    first_cols = pl.ds(0, XFIRST)
    other_cols = pl.ds(XFIRST, width - XFIRST)

    def a_block(zb, lo, count):
        return wbuf.at[pl.ds(lo, count), pl.ds(base_of(zb), depth), first_cols]

    def b_block(xb, zb, lo=0, count=depth):
        return wbuf.at[xb, pl.ds(pl.multiple_of(base_of(zb) + lo, count), count), other_cols]

    def z_of(block):
        if block <= HALF:
            return wrap(z - block, NZ)
        return wrap(z + block - HALF, NZ)

    def a_ring(direction, step, piece):
        zb = wrap(z - (step - 1), NZ) if direction == 0 else wrap(z + (step - 1), NZ)
        part = a_block(zb, piece * (NX // APARTS), NX // APARTS)
        to = right if direction == 0 else left
        at = (direction, step - 1, piece)
        return send(part, part, a_s, a_r.at[at], to, y)

    def t_ring(direction, step):
        zb = wrap(z - (step - 1), NZ) if direction == 0 else wrap(z + (step - 1), NZ)
        part = tab.at[rank, zb]
        to = right if direction == 0 else left
        return send(part, part, t_s, t_r.at[direction, step - 1], to, y)

    def b_ring(direction, step):
        zb = wrap(z - (step - 1), NZ) if direction == 0 else wrap(z + (step - 1), NZ)
        if step < HALF:
            part = b_block(x, zb)
        else:
            part = b_block(x, zb, direction * (depth // 2), depth // 2)
        to = right if direction == 0 else left
        return send(part, part, b_s, b_r.at[direction, step - 1], to, y)

    def b_over_x(block):
        part = b_block(x, z_of(block))
        return [
            send(part, part, bx_s, bx_r.at[way, block], to, y)
            for way, to in ((0, x_next), (1, x_prev))
        ]

    def b_across(block, copies):
        for way, to in ((0, x_next), (1, x_prev)):
            copies[way].wait_recv()
            xb = wrap(x - 1, NX) if way == 0 else wrap(x + 1, NX)
            part = b_block(xb, z_of(block), way * (depth // 2), depth // 2)
            send(part, part, bd_s, bd_r.at[block], to, y)

    def to_sibling(cols, block):
        part = wbuf.at[:, pl.ds(base_of(z_of(block)), depth), cols]
        send(part, part, c_s, c_r, sibling, y)

    wbuf[x, pl.ds(base_of(z), depth), :] = w_ref[...]
    own_first = wbuf.at[x, pl.ds(base_of(z), depth), first_cols]
    for k in range(1, NX):
        send(own_first, own_first, ax_s, ax_r, dp_index(wrap(x + k, NX), z, core), y)
    b_live = {(way, 1): b_ring(way, 1) for way in range(2)}
    over_x = {0: b_over_x(0)}
    hid[y, 0:rows, :] = hq_ref[...]
    hid[y, rows:rows2, :] = hp_ref[...]
    for peer in y_peers:
        send(hid.at[y], hid.at[y], h_s, h_r, me, peer)
    drain(wbuf.at[0, pl.ds(0, (NX - 1) * depth), first_cols], ax_r)
    a_live = {}
    for piece in range(APARTS):
        for way in range(2):
            a_live[way, 1, piece] = a_ring(way, 1, piece)
    to_sibling(first_cols, 0)

    tab[rank, z] = run_table(neg_ref, rows)
    t_live = {(way, 1): t_ring(way, 1) for way in range(2)}

    blocks_of = {0: [0]}
    for step in range(1, HALF):
        blocks_of[step] = [step, HALF + step]
    blocks_of[HALF] = [HALF]

    def finish(step):
        for block in blocks_of[step]:
            drain(b_block(x, z), bd_r.at[block])
            to_sibling(other_cols, block)

    def turn(step):
        for block in blocks_of[step]:
            b_across(block, over_x[block])

    for turn_at in range(1, HALF + 2):
        step = turn_at
        if step <= HALF:
            for way in range(2):
                b_live[way, step].wait_recv()
                if step < HALF:
                    b_live[way, step + 1] = b_ring(way, step + 1)
                    over_x[blocks_of[step][way]] = b_over_x(blocks_of[step][way])
            if step == HALF:
                over_x[HALF] = b_over_x(HALF)
        step = turn_at - 1
        if step >= 1:
            for piece in range(APARTS):
                for way in range(2):
                    if (way, step, piece) not in a_live:
                        continue
                    a_live[way, step, piece].wait_recv()
                    if step + 1 < HALF or (step + 1 == HALF and piece * 2 // APARTS == way):
                        a_live[way, step + 1, piece] = a_ring(way, step + 1, piece)
            for way in range(2):
                if (way, step) in t_live:
                    t_live[way, step].wait_recv()
                    if step + 1 < HALF or (step + 1 == HALF and way == 0):
                        t_live[way, step + 1] = t_ring(way, step + 1)
            for block in blocks_of[step]:
                to_sibling(first_cols, block)
        turn(turn_at - 1)
        if turn_at >= 3:
            finish(turn_at - 3)
    for k, peer in enumerate(mates):
        send(tab.at[rank], tab.at[rank], u_s, u_r, peer, y)
    for step in range(HALF - 1, HALF + 1):
        finish(step)
    drain(wbuf.at[:, pl.ds(0, NZ * depth)], c_r)
    drain(hid.at[pl.ds(0, NY - 1)], h_r)

    tile = width // EPARTS

    def ring(direction, step, piece):
        src_at = 0 if direction == 0 or step == 1 else rows2
        cols = pl.ds(piece * tile, tile)
        src = col.at[step - 1, pl.ds(src_at, rows2), cols]
        if step < HALF:
            dst = col.at[step, pl.ds(direction * rows2, rows2), cols]
        else:
            dst = col.at[0, pl.ds(rows2, rows2), cols]
        to = right if direction == 0 else left
        at = (direction, step - 1, piece)
        return send(src, dst, z_s, z_r.at[at], to, y)

    live = {}
    for piece in range(EPARTS):
        total = jnp.zeros((rows2, tile), F32)
        for b in range(NY):
            total = total + mm(hid[b], wbuf[b, :, piece * tile : (piece + 1) * tile])
        col[0, 0:rows2, piece * tile : (piece + 1) * tile] = total.astype(BF16)
        for direction in range(2):
            live[direction, 1, piece] = ring(direction, 1, piece)
    drain(tab.at[pl.ds(0, NPEER - 1)], u_r)
    fill_picks(tab, sel_ref, rank, z, rows)
    about = about_this(tab, rank, z)

    lane = iota((1, rows2), 1)
    row_id = iota((rows2, rows2), 0)
    lane_id = iota((rows2, rows2), 1)
    eye = row_id == lane_id
    emb = col[0, 0:rows2, :]
    local = lax.rem(pos_ref[...], rows)
    partner = jnp.concatenate([local, local], axis=1).astype(F32)
    partner_col = across(eye, partner).astype(jnp.int32)
    partner = partner.astype(jnp.int32)
    pair = ((lane_id < rows) & (row_id == partner + rows)) | (
        (row_id < rows) & (lane_id == partner_col + rows)
    )
    gram = nt(emb, emb)
    own_sq = down(eye, gram)
    own_pos = down(pair, gram)

    def mask_of(s, r):
        return row_id == idx_ref[s, r : r + 1, :]

    def score(s):
        fill_meets(tab, about, idx_ref, s, rank, z, rows)
        drain(recv.at[s, pl.ds(0, NPEER - 1)], p_r.at[s])
        got = recv[s].reshape(rows2, width)
        cross = nt(emb, got)
        parts = [down(mask_of(s, r), cross) for r in range(RUN)]
        parts += [down(eye, nt(got, got)), own_sq, own_pos, jnp.zeros_like(own_sq)]
        ybuf[y, s] = jnp.concatenate(parts, axis=0)

    pair_rows = iota((2 * rows2, LANES), 0)
    for step in range(1, HALF + 1):
        for piece in range(EPARTS):
            for direction in range(2):
                if (direction, step, piece) not in live:
                    continue
                live[direction, step, piece].wait_recv()
                if step + 1 < HALF or (step + 1 == HALF and piece * 2 // EPARTS == direction):
                    live[direction, step + 1, piece] = ring(direction, step + 1, piece)
        slot = step % HALF
        pick = onehot(pair_rows == sel_ref[slot : slot + 1, :])
        picked = lax.dot_general(
            pick, col[slot], (((0,), (0,)), ((), ())), preferred_element_type=F32
        )
        outbox[slot] = picked.astype(BF16).reshape(NPEER, 2 * KINDS, width)
        for k, peer in enumerate(mates):
            src = outbox.at[slot, wrap(rank + k + 1, NPEER)]
            send(src, recv.at[slot, rank], p_s, p_r.at[slot], peer, y)
        recv[slot, rank] = outbox[slot, rank]
        if step > 1:
            score(step - 1)
    score(0)

    for peer in y_peers:
        send(ybuf.at[y], ybuf.at[y], y_s, y_r, me, peer)
    drain(ybuf.at[pl.ds(0, NY - 1)], y_r)

    sums = [((ybuf[0, s] + ybuf[1, s]) + ybuf[2, s]) + ybuf[3, s] for s in range(HALF)]
    inv_row = 1.0 / jnp.sqrt(sums[0][5:6] + EPS)
    inv_col = across(eye, inv_row)
    pos_score = SCALE * sums[0][6:7] * inv_row * down(pair, inv_col)
    pos_exp = jnp.exp(pos_score)
    denom = across(eye, pos_exp)
    scores = []
    exps = []
    lane_inv = []
    for d in range(HALF):
        rl = 1.0 / jnp.sqrt(sums[d][4:5] + EPS)
        lane_inv.append(rl)
        sc = []
        ex = []
        for r in range(RUN):
            mask = mask_of(d, r)
            s = SCALE * sums[d][r : r + 1] * rl * down(mask, inv_col)
            e = jnp.exp(s)
            sc.append(s)
            ex.append(e)
            denom = denom + across(mask, e)
        scores.append(sc)
        exps.append(ex)
    denom_row = down(eye, denom)
    loss_ref[...] = jnp.log(denom_row[:, 0:rows]) - pos_score[:, 0:rows]
    is_query = lane < rows
    dinv_row = jnp.where(is_query, 1.0 / denom_row, 0.0)
    dinv_col = across(eye, dinv_row)

    dz[0] = dinv_row
    for k, peer in enumerate(z_peers):
        send(dz.at[0], dz.at[k + 1], d_s, d_r, peer, y)

    pos_coef = jnp.where(is_query, SCALE * (pos_exp * dinv_row - 1.0), 0.0)
    pos_coef = pos_coef + down(pair, across(eye, pos_coef))

    def half(part):
        return slice(part * rows, (part + 1) * rows)

    def half_weights(part, dinv_at):
        half_id = iota((rows, rows2), 0) + part * rows
        weights = []
        inners = []
        for s in range(HALF):
            weight = jnp.zeros((rows, rows2), F32)
            inner = jnp.zeros((rows, rows2), F32)
            for r in range(RUN):
                mask = half_id == idx_ref[s, r : r + 1, :]
                coef = exps[s][r] * dinv_at(s, r)
                weight = weight + jnp.where(mask, SCALE * coef * lane_inv[s], 0.0)
                inner = inner + jnp.where(mask, coef * scores[s][r], 0.0)
            weights.append(weight)
            inners.append(inner)
        return weights, inners

    def half_grads(part, weights, inner):
        def weighted(weight, values):
            high = weight.astype(BF16)
            low = (weight - high.astype(F32)).astype(BF16)
            term = mm(jnp.concatenate([high, low], axis=0), values)
            return term[0:rows] + term[rows:]

        half_pair = pair[half(part)]
        inner = jnp.sum(inner, axis=1, keepdims=True)
        inner = inner + across(half_pair, pos_coef * pos_score * (1.0 / SCALE))
        arrived = recv[...].reshape(HALF * rows2, width)
        acc[...] = weighted(jnp.where(half_pair, pos_coef * inv_row, 0.0), emb) + weighted(
            jnp.concatenate(weights, axis=1), arrived
        )
        unit = emb[half(part)].astype(F32) * inv_col[half(part)]
        return ((acc[...] - unit * inner) * inv_col[half(part)]).astype(BF16)

    def project(part, g_emb):
        for k in (2, 1, 3, NY):
            block = wrap(y + k, NY)
            gpart[part, k - 1] = nt(g_emb, wbuf[block]).astype(BF16)
            if k < NY:
                mine = gpart.at[part, k - 1]
                theirs = gin.at[part, k - 1]
                send(mine, theirs, g_s, g_r.at[part], me, block)

    def gathered(part):
        total = gpart[part, NY - 1].astype(F32)
        drain(gin.at[part], g_r.at[part])
        for k in range(NY - 1):
            total = total + gin[part, k].astype(F32)
        return total.astype(BF16)

    weights, inners = half_weights(0, lambda s, r: down(mask_of(s, r), dinv_col))
    g_query = half_grads(0, weights, sum(inners))
    drain(dz.at[pl.ds(0, NZ - 1)], d_r)
    for k, peer in enumerate(mates):
        send(dz, dtab.at[k + 1], e_s, e_r, peer, y)
    for k in range(NZ):
        dtab[0, k] = dz[k]
    project(0, g_query)

    weights, inners = half_weights(1, lambda s, r: 1.0)
    drain(dtab.at[pl.ds(0, NPEER - 1)], e_r)
    at_source = iota((NZ, rows2), 0) == lax.div(iota((NZ, rows2), 1), KINDS)
    inner = jnp.zeros((rows, rows2), F32)
    for s in range(HALF):
        ahead = (s, NZ - s) if s else (0, HALF)
        table = [dtab[wrap(rank - d, NPEER), k] for d in range(NPEER) for k in ahead]
        table = jnp.concatenate(table, axis=0)
        high = table.astype(BF16)
        rest = table - high.astype(F32)
        middle = rest.astype(BF16)
        low = (rest - middle.astype(F32)).astype(BF16)
        spread = onehot(row_id == idx_ref[s, RUN : RUN + 1, :])
        found = mm(jnp.concatenate([high, middle, low], axis=0), spread)
        found = (found[0:NZ] + found[NZ : 2 * NZ]) + found[2 * NZ :]
        their_inv = down(at_source, found)
        weights[s] = weights[s] * their_inv
        inner = inner + inners[s] * their_inv
    project(1, half_grads(1, weights, inner))
    gq_ref[...] = gathered(0)
    gp_ref[...] = gathered(1)

    drain(hid.at[pl.ds(0, NY - 1)], h_s)
    drain(tab.at[0, pl.ds(0, NZ - 1)], t_s)
    drain(tab.at[pl.ds(0, NPEER - 1)], u_s)
    drain(wbuf.at[:, pl.ds(0, (NZ - 1) * depth), first_cols], a_s)
    drain(wbuf.at[0, pl.ds(0, (NZ - 1) * depth), other_cols], b_s)
    drain(wbuf.at[0, pl.ds(0, (NX - 1) * depth), first_cols], ax_s)
    drain(wbuf.at[0, pl.ds(0, 2 * NZ * depth), other_cols], bx_s)
    drain(wbuf.at[0, pl.ds(0, NZ * depth), other_cols], bd_s)
    drain(wbuf.at[:, pl.ds(0, NZ * depth)], c_s)
    drain(col.at[:, pl.ds(0, rows2 * (NZ - 1) // HALF)], z_s)
    drain(outbox.at[:, pl.ds(0, NPEER - 1)], p_s)
    drain(ybuf.at[pl.ds(0, NY - 1)], y_s)
    drain(dz.at[pl.ds(0, NZ - 1)], d_s)
    drain(dtab.at[pl.ds(0, NPEER - 1)], e_s)
    drain(gin, g_s)


def body(q_hidden, p_hidden, proj, positives, negatives):
    rows, width = q_hidden.shape
    rows2 = 2 * rows
    block = proj.shape[0] * NDP // NX
    vmem = pl.BlockSpec(memory_space=pltpu.VMEM)
    dma = pltpu.SemaphoreType.DMA

    grad_q, grad_p, loss = pl.pallas_call(
        fused_kernel,
        out_shape=(
            jax.ShapeDtypeStruct((rows, width), BF16),
            jax.ShapeDtypeStruct((rows, width), BF16),
            jax.ShapeDtypeStruct((1, rows), F32),
        ),
        in_specs=[vmem] * 5,
        out_specs=(vmem,) * 3,
        scratch_shapes=[
            pltpu.VMEM((NY, rows2, width), BF16),
            pltpu.VMEM((NX, block, width), BF16),
            pltpu.VMEM((NPEER, NZ, 8, LANES), F32),
            pltpu.VMEM((HALF, LANES), jnp.int32),
            pltpu.VMEM((HALF, 8, LANES), jnp.int32),
            pltpu.VMEM((HALF, 2 * rows2, width), BF16),
            pltpu.VMEM((HALF, NPEER, 2 * KINDS, width), BF16),
            pltpu.VMEM((HALF, NPEER, 2 * KINDS, width), BF16),
            pltpu.VMEM((NY, NPEER, 8, rows2), F32),
            pltpu.VMEM((NZ, 1, rows2), F32),
            pltpu.VMEM((NPEER, NZ, 1, rows2), F32),
            pltpu.VMEM((2, NY, rows, width), BF16),
            pltpu.VMEM((2, NY - 1, rows, width), BF16),
            pltpu.VMEM((rows, width), F32),
        ]
        + [dma, dma]
        + [dma, dma((2, HALF))]
        + [dma, dma]
        + [dma, dma((2, HALF, APARTS))]
        + [dma, dma((2, HALF))]
        + [dma, dma]
        + [dma, dma((2, NZ))]
        + [dma, dma((NZ,))]
        + [dma, dma]
        + [dma, dma((2, HALF, EPARTS))]
        + [dma, dma((HALF,))]
        + [dma, dma]
        + [dma, dma]
        + [dma, dma]
        + [dma, dma((2,))],
        compiler_params=pltpu.CompilerParams(
            collective_id=0, has_side_effects=True, vmem_limit_bytes=56 * 1024 * 1024
        ),
        cost_estimate=pl.CostEstimate(
            flops=3 * 10**9, bytes_accessed=10**8, transcendentals=10**5
        ),
        name="contrastive_backward",
    )(q_hidden, p_hidden, proj, negatives.T, positives[None, :])
    return (grad_q, grad_p, loss[0])


def solution(mesh):
    placed = (P("dp", "mp"), P("dp", "mp"), P("dp", "mp"), P("dp"), P("dp", None))
    return jax.shard_map(
        body,
        mesh=mesh,
        in_specs=placed,
        out_specs=(P("dp", "mp"), P("dp", "mp"), P("dp")),
        check_vma=False,
    )
```

```python
import functools

import jax
import jax.numpy as jnp
from jax import lax
from jax.experimental import pallas as pl
from jax.experimental.pallas import tpu as pltpu
from jax.sharding import PartitionSpec as P

SCALE = 20.0
EPS = 1e-06
MESH = pl.DeviceIdType.MESH
F32 = jnp.float32
BF16 = jnp.bfloat16

NX, NZ, NC, NY = 4, 16, 2, 4
NDP = NX * NZ * NC
NPEER = NX * NC
HALF = NZ // 2
RUN = 4
CAP = 3
LANES = 128
XFIRST = 256
APARTS = 4
EPARTS = 4
KINDS = 8


def coords():
    dp = lax.axis_index("dp")
    y = lax.axis_index("mp")
    core = lax.rem(dp, NC)
    chip = lax.div(dp, NC)
    return lax.div(chip, NZ), y, lax.rem(chip, NZ), core


def dp_index(x, z, core):
    return (x * NZ + z) * NC + core


def wrap(value, size):
    return lax.rem(value + 2 * size, size)


def remote(src, dst, send_sem, recv_sem, dp, y):
    return pltpu.make_async_remote_copy(
        src_ref=src,
        dst_ref=dst,
        send_sem=send_sem,
        recv_sem=recv_sem,
        device_id=(dp, y),
        device_id_type=MESH,
    )


def nt(a, b):
    return lax.dot_general(a, b, (((1,), (1,)), ((), ())), preferred_element_type=F32)


def mm(a, b):
    return jnp.dot(a, b, preferred_element_type=F32)


def onehot(mask):
    return jnp.where(mask, 1.0, 0.0).astype(BF16)


def iota(shape, dim):
    return lax.broadcasted_iota(jnp.int32, shape, dim)


def down(mask, value):
    return jnp.sum(jnp.where(mask, value, 0.0), axis=0, keepdims=True)


def across(mask, value):
    return jnp.sum(jnp.where(mask, value, 0.0), axis=1, keepdims=True)


def greet(peers):
    barrier = pltpu.get_barrier_semaphore()
    for dp, y in peers:
        pl.semaphore_signal(barrier, inc=1, device_id=(dp, y), device_id_type=MESH)
    pl.semaphore_wait(barrier, len(peers))


def run_table(neg_ref, rows):
    holder = iota((rows, LANES), 1)
    query = iota((rows, LANES), 0).astype(F32)
    holder = dp_index(
        lax.div(holder, NZ * NC), lax.rem(holder, NZ), lax.rem(lax.div(holder, NZ), NC)
    ).astype(F32)
    before = onehot(iota((rows, rows), 1) < iota((rows, rows), 0))
    base = jnp.zeros((1, LANES), F32)
    passages = [base] * RUN
    queries = [base] * CAP
    ids = neg_ref[...]
    turn = onehot(iota((rows, rows), 0) == iota((rows, rows), 1))
    owners = nt(turn, lax.div(ids, rows).astype(F32).astype(BF16))
    locals_ = nt(turn, lax.rem(ids, rows).astype(F32).astype(BF16))
    for r in range(neg_ref.shape[0] // RUN):
        hit = owners[:, RUN * r : RUN * r + 1] == holder
        rank = mm(before, onehot(hit)) + base
        base = base + jnp.sum(jnp.where(hit, 1.0, 0.0), axis=0, keepdims=True)
        for i in range(CAP):
            queries[i] = queries[i] + down(hit & (rank == float(i)), query + 1.0)
        for j in range(RUN):
            local = locals_[:, RUN * r + j : RUN * r + j + 1]
            named = jnp.max(jnp.where(hit, local, 0.0), axis=0, keepdims=True)
            passages[j] = jnp.maximum(passages[j], named)
    return jnp.concatenate(passages + [q - 1.0 for q in queries] + [jnp.full((1, LANES), -1.0)], 0)


def seen_z(z, step, second):
    ahead = jnp.where(step == 0, HALF, step)
    return lax.rem(jnp.where(second == 0, z - step + NZ, z + ahead), NZ)


def fill_picks(tab, sel_ref, rank, z, rows):
    lane8 = iota((NPEER, LANES), 1)
    row8 = iota((NPEER, LANES), 0)
    row = iota((LANES, LANES), 0)
    lane = iota((LANES, LANES), 1)
    kind = lax.rem(lane8, KINDS)
    second = lax.rem(lax.div(lane8, KINDS), 2)
    kind_l = lax.rem(lane, KINDS)
    second_l = lax.rem(lax.div(lane, KINDS), 2)
    group_l = lax.div(lane, 2 * KINDS)
    asked = jnp.concatenate([tab[d, z] for d in range(NPEER) for _ in range(2)], axis=0).astype(BF16)
    zero8 = jnp.zeros_like(row8)
    firsts = nt(onehot(lane8 == rank * NZ + seen_z(z, row8, zero8)), asked)
    seconds = nt(onehot(lane8 == rank * NZ + seen_z(z, row8, zero8 + 1)), asked)
    from_p = jnp.where(second == 0, firsts, seconds) + float(rows)
    here = tab[rank].reshape(LANES, LANES).astype(BF16)
    spread = mm(here, onehot(row == group_l * NZ + z))
    from_q = jnp.concatenate(
        [
            down(row == seen_z(z, jnp.full_like(lane, s), second_l) * KINDS + kind_l, spread)
            for s in range(HALF)
        ],
        axis=0,
    )
    picked = jnp.where(kind < RUN, from_p, from_q)
    picked = jnp.where(picked >= 0.0, picked + (second * 2 * rows).astype(F32), -1.0)
    sel_ref[...] = picked.astype(jnp.int32)


def about_this(tab, rank, z):
    lane8 = iota((NPEER, LANES), 1)
    row = iota((LANES, LANES), 0)
    lane = iota((LANES, LANES), 1)
    me_row = onehot(lane8 == rank * NZ + z)
    said = [nt(me_row, tab[d].reshape(LANES, LANES).astype(BF16))[0:1] for d in range(NPEER)]
    said = jnp.concatenate(said, axis=0)
    low = said.astype(BF16)
    first = lane - lax.rem(lane, KINDS)
    passages = [mm(low, onehot(row == first + r)) for r in range(RUN)]
    return jnp.concatenate([said] + passages, axis=0).astype(BF16)


def fill_meets(tab, about, idx_ref, step, rank, z, rows):
    row = iota((LANES, LANES), 0)
    lane = iota((LANES, LANES), 1)
    kind_l = lax.rem(lane, KINDS)
    group_l = lax.div(lane, 2 * KINDS)
    z_l = seen_z(z, jnp.full_like(lane, step), lax.rem(lax.div(lane, KINDS), 2))
    kind = kind_l[0:1]
    own = mm(tab[rank, z].astype(BF16), onehot(row == group_l * NZ + z_l))
    found = mm(about, onehot(row == z_l * KINDS + kind_l))
    from_peer = row[0:NPEER] == group_l[0:NPEER]
    picked = [down(from_peer, found[NPEER * k : NPEER * (k + 1)]) for k in range(RUN + 1)]
    wants = picked[0]
    out = []
    for r in range(RUN):
        theirs = jnp.where(wants >= 0.0, picked[1 + r] + float(rows), -1.0)
        out.append(jnp.where(kind < RUN, own[RUN + r : RUN + r + 1], theirs))
    out.append(jnp.where(kind < RUN, -1.0, wants))
    out += [jnp.full((1, LANES), -1.0)] * (8 - len(out))
    idx_ref[step] = jnp.concatenate(out, axis=0).astype(jnp.int32)


def fused_kernel(
    hq_ref,
    hp_ref,
    w_ref,
    neg_ref,
    pos_ref,
    gq_ref,
    gp_ref,
    loss_ref,
    hid,
    wbuf,
    tab,
    sel_ref,
    idx_ref,
    col,
    outbox,
    recv,
    ybuf,
    dz,
    dtab,
    gpart,
    gin,
    acc,
    h_s,
    h_r,
    t_s,
    t_r,
    u_s,
    u_r,
    a_s,
    a_r,
    b_s,
    b_r,
    ax_s,
    ax_r,
    bx_s,
    bx_r,
    bd_s,
    bd_r,
    c_s,
    c_r,
    z_s,
    z_r,
    p_s,
    p_r,
    y_s,
    y_r,
    d_s,
    d_r,
    e_s,
    e_r,
    g_s,
    g_r,
):
    x, y, z, core = coords()
    me = dp_index(x, z, core)
    rank = x * NC + core
    rows, width = hq_ref.shape
    rows2 = 2 * rows
    depth = w_ref.shape[0]
    right = dp_index(x, wrap(z + 1, NZ), core)
    left = dp_index(x, wrap(z - 1, NZ), core)
    x_next = dp_index(wrap(x + 1, NX), z, core)
    x_prev = dp_index(wrap(x - 1, NX), z, core)
    sibling = dp_index(x, z, 1 - core)

    def peer_of(k):
        other = wrap(rank + k, NPEER)
        return dp_index(lax.div(other, NC), z, lax.rem(other, NC))

    y_peers = [wrap(y + k, NY) for k in range(1, NY)]
    z_peers = [dp_index(x, wrap(z + k, NZ), core) for k in range(1, NZ)]
    mates = [peer_of(k) for k in range(1, NPEER)]
    greet([(me, p) for p in y_peers] + [(right, y), (left, y)] + [(p, y) for p in mates])

    def send(src, dst, send_sem, recv_sem, dp, at_y):
        cp = remote(src, dst, send_sem, recv_sem, dp, at_y)
        cp.start()
        return cp

    def drain(ref, sem):
        pltpu.make_async_copy(ref, ref, sem).wait()

    def base_of(zb):
        return pl.multiple_of((zb * NC + core) * depth, depth)

    first_cols = pl.ds(0, XFIRST)
    other_cols = pl.ds(XFIRST, width - XFIRST)

    def a_block(zb, lo, count):
        return wbuf.at[pl.ds(lo, count), pl.ds(base_of(zb), depth), first_cols]

    def b_block(xb, zb, lo=0, count=depth):
        return wbuf.at[xb, pl.ds(pl.multiple_of(base_of(zb) + lo, count), count), other_cols]

    def z_of(block):
        if block <= HALF:
            return wrap(z - block, NZ)
        return wrap(z + block - HALF, NZ)

    def a_ring(direction, step, piece):
        zb = wrap(z - (step - 1), NZ) if direction == 0 else wrap(z + (step - 1), NZ)
        part = a_block(zb, piece * (NX // APARTS), NX // APARTS)
        to = right if direction == 0 else left
        at = (direction, step - 1, piece)
        return send(part, part, a_s, a_r.at[at], to, y)

    def t_ring(direction, step):
        zb = wrap(z - (step - 1), NZ) if direction == 0 else wrap(z + (step - 1), NZ)
        part = tab.at[rank, zb]
        to = right if direction == 0 else left
        return send(part, part, t_s, t_r.at[direction, step - 1], to, y)

    def b_ring(direction, step):
        zb = wrap(z - (step - 1), NZ) if direction == 0 else wrap(z + (step - 1), NZ)
        if step < HALF:
            part = b_block(x, zb)
        else:
            part = b_block(x, zb, direction * (depth // 2), depth // 2)
        to = right if direction == 0 else left
        return send(part, part, b_s, b_r.at[direction, step - 1], to, y)

    def b_over_x(block):
        part = b_block(x, z_of(block))
        return [
            send(part, part, bx_s, bx_r.at[way, block], to, y)
            for way, to in ((0, x_next), (1, x_prev))
        ]

    def b_across(block, copies):
        for way, to in ((0, x_next), (1, x_prev)):
            copies[way].wait_recv()
            xb = wrap(x - 1, NX) if way == 0 else wrap(x + 1, NX)
            part = b_block(xb, z_of(block), way * (depth // 2), depth // 2)
            send(part, part, bd_s, bd_r.at[block], to, y)

    def to_sibling(cols, block):
        part = wbuf.at[:, pl.ds(base_of(z_of(block)), depth), cols]
        send(part, part, c_s, c_r, sibling, y)

    wbuf[x, pl.ds(base_of(z), depth), :] = w_ref[...]
    own_first = wbuf.at[x, pl.ds(base_of(z), depth), first_cols]
    for k in range(1, NX):
        send(own_first, own_first, ax_s, ax_r, dp_index(wrap(x + k, NX), z, core), y)
    b_live = {(way, 1): b_ring(way, 1) for way in range(2)}
    over_x = {0: b_over_x(0)}
    hid[y, 0:rows, :] = hq_ref[...]
    hid[y, rows:rows2, :] = hp_ref[...]
    for peer in y_peers:
        send(hid.at[y], hid.at[y], h_s, h_r, me, peer)
    drain(wbuf.at[0, pl.ds(0, (NX - 1) * depth), first_cols], ax_r)
    a_live = {}
    for piece in range(APARTS):
        for way in range(2):
            a_live[way, 1, piece] = a_ring(way, 1, piece)
    to_sibling(first_cols, 0)

    tab[rank, z] = run_table(neg_ref, rows)
    t_live = {(way, 1): t_ring(way, 1) for way in range(2)}

    blocks_of = {0: [0]}
    for step in range(1, HALF):
        blocks_of[step] = [step, HALF + step]
    blocks_of[HALF] = [HALF]

    def finish(step):
        for block in blocks_of[step]:
            drain(b_block(x, z), bd_r.at[block])
            to_sibling(other_cols, block)

    def turn(step):
        for block in blocks_of[step]:
            b_across(block, over_x[block])

    for turn_at in range(1, HALF + 2):
        step = turn_at
        if step <= HALF:
            for way in range(2):
                b_live[way, step].wait_recv()
                if step < HALF:
                    b_live[way, step + 1] = b_ring(way, step + 1)
                    over_x[blocks_of[step][way]] = b_over_x(blocks_of[step][way])
            if step == HALF:
                over_x[HALF] = b_over_x(HALF)
        step = turn_at - 1
        if step >= 1:
            for piece in range(APARTS):
                for way in range(2):
                    if (way, step, piece) not in a_live:
                        continue
                    a_live[way, step, piece].wait_recv()
                    if step + 1 < HALF or (step + 1 == HALF and piece * 2 // APARTS == way):
                        a_live[way, step + 1, piece] = a_ring(way, step + 1, piece)
            for way in range(2):
                if (way, step) in t_live:
                    t_live[way, step].wait_recv()
                    if step + 1 < HALF or (step + 1 == HALF and way == 0):
                        t_live[way, step + 1] = t_ring(way, step + 1)
            for block in blocks_of[step]:
                to_sibling(first_cols, block)
        turn(turn_at - 1)
        if turn_at >= 3:
            finish(turn_at - 3)
    for k, peer in enumerate(mates):
        send(tab.at[rank], tab.at[rank], u_s, u_r, peer, y)
    for step in range(HALF - 1, HALF + 1):
        finish(step)
    drain(wbuf.at[:, pl.ds(0, NZ * depth)], c_r)
    drain(hid.at[pl.ds(0, NY - 1)], h_r)

    tile = width // EPARTS

    def ring(direction, step, piece):
        src_at = 0 if direction == 0 or step == 1 else rows2
        cols = pl.ds(piece * tile, tile)
        src = col.at[step - 1, pl.ds(src_at, rows2), cols]
        if step < HALF:
            dst = col.at[step, pl.ds(direction * rows2, rows2), cols]
        else:
            dst = col.at[0, pl.ds(rows2, rows2), cols]
        to = right if direction == 0 else left
        at = (direction, step - 1, piece)
        return send(src, dst, z_s, z_r.at[at], to, y)

    live = {}
    for piece in range(EPARTS):
        total = jnp.zeros((rows2, tile), F32)
        for b in range(NY):
            total = total + mm(hid[b], wbuf[b, :, piece * tile : (piece + 1) * tile])
        col[0, 0:rows2, piece * tile : (piece + 1) * tile] = total.astype(BF16)
        for direction in range(2):
            live[direction, 1, piece] = ring(direction, 1, piece)
    lane = iota((1, rows2), 1)
    row_id = iota((rows2, rows2), 0)
    lane_id = iota((rows2, rows2), 1)
    eye = row_id == lane_id
    emb = col[0, 0:rows2, :]
    local = lax.rem(pos_ref[...], rows)
    partner = jnp.concatenate([local, local], axis=1).astype(F32)
    partner_col = across(eye, partner).astype(jnp.int32)
    partner = partner.astype(jnp.int32)
    pair = ((lane_id < rows) & (row_id == partner + rows)) | (
        (row_id < rows) & (lane_id == partner_col + rows)
    )

    def mask_of(s, r):
        return row_id == idx_ref[s, r : r + 1, :]

    def score(s):
        fill_meets(tab, about, idx_ref, s, rank, z, rows)
        drain(recv.at[s, pl.ds(0, NPEER - 1)], p_r.at[s])
        got = recv[s].reshape(rows2, width)
        cross = nt(emb, got)
        parts = [down(mask_of(s, r), cross) for r in range(RUN)]
        parts += [down(eye, nt(got, got)), own_sq, own_pos, jnp.zeros_like(own_sq)]
        ybuf[y, s] = jnp.concatenate(parts, axis=0)

    pair_rows = iota((2 * rows2, LANES), 0)
    for step in range(1, HALF + 1):
        for piece in range(EPARTS):
            for direction in range(2):
                if (direction, step, piece) not in live:
                    continue
                live[direction, step, piece].wait_recv()
                if step + 1 < HALF or (step + 1 == HALF and piece * 2 // EPARTS == direction):
                    live[direction, step + 1, piece] = ring(direction, step + 1, piece)
        if step == 1:
            drain(tab.at[pl.ds(0, NPEER - 1)], u_r)
            fill_picks(tab, sel_ref, rank, z, rows)
            about = about_this(tab, rank, z)
            gram = nt(emb, emb)
            own_sq = down(eye, gram)
            own_pos = down(pair, gram)
        slot = step % HALF
        pick = onehot(pair_rows == sel_ref[slot : slot + 1, :])
        picked = lax.dot_general(
            pick, col[slot], (((0,), (0,)), ((), ())), preferred_element_type=F32
        )
        outbox[slot] = picked.astype(BF16).reshape(NPEER, 2 * KINDS, width)
        for k, peer in enumerate(mates):
            src = outbox.at[slot, wrap(rank + k + 1, NPEER)]
            send(src, recv.at[slot, rank], p_s, p_r.at[slot], peer, y)
        recv[slot, rank] = outbox[slot, rank]
        if step > 1:
            score(step - 1)
    score(0)

    for peer in y_peers:
        send(ybuf.at[y], ybuf.at[y], y_s, y_r, me, peer)
    drain(ybuf.at[pl.ds(0, NY - 1)], y_r)

    sums = [((ybuf[0, s] + ybuf[1, s]) + ybuf[2, s]) + ybuf[3, s] for s in range(HALF)]
    inv_row = 1.0 / jnp.sqrt(sums[0][5:6] + EPS)
    inv_col = across(eye, inv_row)
    pos_score = SCALE * sums[0][6:7] * inv_row * down(pair, inv_col)
    pos_exp = jnp.exp(pos_score)
    denom = across(eye, pos_exp)
    scores = []
    exps = []
    lane_inv = []
    for d in range(HALF):
        rl = 1.0 / jnp.sqrt(sums[d][4:5] + EPS)
        lane_inv.append(rl)
        sc = []
        ex = []
        for r in range(RUN):
            mask = mask_of(d, r)
            s = SCALE * sums[d][r : r + 1] * rl * down(mask, inv_col)
            e = jnp.exp(s)
            sc.append(s)
            ex.append(e)
            denom = denom + across(mask, e)
        scores.append(sc)
        exps.append(ex)
    denom_row = down(eye, denom)
    loss_ref[...] = jnp.log(denom_row[:, 0:rows]) - pos_score[:, 0:rows]
    is_query = lane < rows
    dinv_row = jnp.where(is_query, 1.0 / denom_row, 0.0)
    dinv_col = across(eye, dinv_row)

    dz[0] = dinv_row
    for k, peer in enumerate(z_peers):
        send(dz.at[0], dz.at[k + 1], d_s, d_r, peer, y)

    pos_coef = jnp.where(is_query, SCALE * (pos_exp * dinv_row - 1.0), 0.0)
    pos_coef = pos_coef + down(pair, across(eye, pos_coef))

    def half(part):
        return slice(part * rows, (part + 1) * rows)

    def half_weights(part, dinv_at):
        half_id = iota((rows, rows2), 0) + part * rows
        weights = []
        inners = []
        for s in range(HALF):
            weight = jnp.zeros((rows, rows2), F32)
            inner = jnp.zeros((rows, rows2), F32)
            for r in range(RUN):
                mask = half_id == idx_ref[s, r : r + 1, :]
                coef = exps[s][r] * dinv_at(s, r)
                weight = weight + jnp.where(mask, SCALE * coef * lane_inv[s], 0.0)
                inner = inner + jnp.where(mask, coef * scores[s][r], 0.0)
            weights.append(weight)
            inners.append(inner)
        return weights, inners

    def half_grads(part, weights, inner):
        def weighted(weight, values):
            high = weight.astype(BF16)
            low = (weight - high.astype(F32)).astype(BF16)
            term = mm(jnp.concatenate([high, low], axis=0), values)
            return term[0:rows] + term[rows:]

        half_pair = pair[half(part)]
        inner = jnp.sum(inner, axis=1, keepdims=True)
        inner = inner + across(half_pair, pos_coef * pos_score * (1.0 / SCALE))
        arrived = recv[...].reshape(HALF * rows2, width)
        acc[...] = weighted(jnp.where(half_pair, pos_coef * inv_row, 0.0), emb) + weighted(
            jnp.concatenate(weights, axis=1), arrived
        )
        unit = emb[half(part)].astype(F32) * inv_col[half(part)]
        return ((acc[...] - unit * inner) * inv_col[half(part)]).astype(BF16)

    def project(part, g_emb):
        for k in (2, 1, 3, NY):
            block = wrap(y + k, NY)
            gpart[part, k - 1] = nt(g_emb, wbuf[block]).astype(BF16)
            if k < NY:
                mine = gpart.at[part, k - 1]
                theirs = gin.at[part, k - 1]
                send(mine, theirs, g_s, g_r.at[part], me, block)

    def gathered(part):
        total = gpart[part, NY - 1].astype(F32)
        drain(gin.at[part], g_r.at[part])
        for k in range(NY - 1):
            total = total + gin[part, k].astype(F32)
        return total.astype(BF16)

    weights, inners = half_weights(0, lambda s, r: down(mask_of(s, r), dinv_col))
    g_query = half_grads(0, weights, sum(inners))
    weights, inners = half_weights(1, lambda s, r: 1.0)
    drain(dz.at[pl.ds(0, NZ - 1)], d_r)
    for k, peer in enumerate(mates):
        send(dz, dtab.at[k + 1], e_s, e_r, peer, y)
    for k in range(NZ):
        dtab[0, k] = dz[k]
    project(0, g_query)

    drain(dtab.at[pl.ds(0, NPEER - 1)], e_r)
    at_source = iota((NZ, rows2), 0) == lax.div(iota((NZ, rows2), 1), KINDS)
    inner = jnp.zeros((rows, rows2), F32)
    for s in range(HALF):
        ahead = (s, NZ - s) if s else (0, HALF)
        table = [dtab[wrap(rank - d, NPEER), k] for d in range(NPEER) for k in ahead]
        table = jnp.concatenate(table, axis=0)
        high = table.astype(BF16)
        rest = table - high.astype(F32)
        middle = rest.astype(BF16)
        low = (rest - middle.astype(F32)).astype(BF16)
        spread = onehot(row_id == idx_ref[s, RUN : RUN + 1, :])
        found = mm(jnp.concatenate([high, middle, low], axis=0), spread)
        found = (found[0:NZ] + found[NZ : 2 * NZ]) + found[2 * NZ :]
        their_inv = down(at_source, found)
        weights[s] = weights[s] * their_inv
        inner = inner + inners[s] * their_inv
    project(1, half_grads(1, weights, inner))
    gq_ref[...] = gathered(0)
    gp_ref[...] = gathered(1)

    drain(hid.at[pl.ds(0, NY - 1)], h_s)
    drain(tab.at[0, pl.ds(0, NZ - 1)], t_s)
    drain(tab.at[pl.ds(0, NPEER - 1)], u_s)
    drain(wbuf.at[:, pl.ds(0, (NZ - 1) * depth), first_cols], a_s)
    drain(wbuf.at[0, pl.ds(0, (NZ - 1) * depth), other_cols], b_s)
    drain(wbuf.at[0, pl.ds(0, (NX - 1) * depth), first_cols], ax_s)
    drain(wbuf.at[0, pl.ds(0, 2 * NZ * depth), other_cols], bx_s)
    drain(wbuf.at[0, pl.ds(0, NZ * depth), other_cols], bd_s)
    drain(wbuf.at[:, pl.ds(0, NZ * depth)], c_s)
    drain(col.at[:, pl.ds(0, rows2 * (NZ - 1) // HALF)], z_s)
    drain(outbox.at[:, pl.ds(0, NPEER - 1)], p_s)
    drain(ybuf.at[pl.ds(0, NY - 1)], y_s)
    drain(dz.at[pl.ds(0, NZ - 1)], d_s)
    drain(dtab.at[pl.ds(0, NPEER - 1)], e_s)
    drain(gin, g_s)


def body(q_hidden, p_hidden, proj, positives, negatives):
    rows, width = q_hidden.shape
    rows2 = 2 * rows
    block = proj.shape[0] * NDP // NX
    vmem = pl.BlockSpec(memory_space=pltpu.VMEM)
    dma = pltpu.SemaphoreType.DMA

    grad_q, grad_p, loss = pl.pallas_call(
        fused_kernel,
        out_shape=(
            jax.ShapeDtypeStruct((rows, width), BF16),
            jax.ShapeDtypeStruct((rows, width), BF16),
            jax.ShapeDtypeStruct((1, rows), F32),
        ),
        in_specs=[vmem] * 5,
        out_specs=(vmem,) * 3,
        scratch_shapes=[
            pltpu.VMEM((NY, rows2, width), BF16),
            pltpu.VMEM((NX, block, width), BF16),
            pltpu.VMEM((NPEER, NZ, 8, LANES), F32),
            pltpu.VMEM((HALF, LANES), jnp.int32),
            pltpu.VMEM((HALF, 8, LANES), jnp.int32),
            pltpu.VMEM((HALF, 2 * rows2, width), BF16),
            pltpu.VMEM((HALF, NPEER, 2 * KINDS, width), BF16),
            pltpu.VMEM((HALF, NPEER, 2 * KINDS, width), BF16),
            pltpu.VMEM((NY, NPEER, 8, rows2), F32),
            pltpu.VMEM((NZ, 1, rows2), F32),
            pltpu.VMEM((NPEER, NZ, 1, rows2), F32),
            pltpu.VMEM((2, NY, rows, width), BF16),
            pltpu.VMEM((2, NY - 1, rows, width), BF16),
            pltpu.VMEM((rows, width), F32),
        ]
        + [dma, dma]
        + [dma, dma((2, HALF))]
        + [dma, dma]
        + [dma, dma((2, HALF, APARTS))]
        + [dma, dma((2, HALF))]
        + [dma, dma]
        + [dma, dma((2, NZ))]
        + [dma, dma((NZ,))]
        + [dma, dma]
        + [dma, dma((2, HALF, EPARTS))]
        + [dma, dma((HALF,))]
        + [dma, dma]
        + [dma, dma]
        + [dma, dma]
        + [dma, dma((2,))],
        compiler_params=pltpu.CompilerParams(
            collective_id=0, has_side_effects=True, vmem_limit_bytes=56 * 1024 * 1024
        ),
        cost_estimate=pl.CostEstimate(
            flops=3 * 10**9, bytes_accessed=10**8, transcendentals=10**5
        ),
        name="contrastive_backward",
    )(q_hidden, p_hidden, proj, negatives.T, positives[None, :])
    return (grad_q, grad_p, loss[0])


def solution(mesh):
    placed = (P("dp", "mp"), P("dp", "mp"), P("dp", "mp"), P("dp"), P("dp", None))
    return jax.shard_map(
        body,
        mesh=mesh,
        in_specs=placed,
        out_specs=(P("dp", "mp"), P("dp", "mp"), P("dp")),
        check_vma=False,
    )
```

```python
import functools

import jax
import jax.numpy as jnp
from jax import lax
from jax.experimental import pallas as pl
from jax.experimental.pallas import tpu as pltpu
from jax.sharding import PartitionSpec as P

SCALE = 20.0
EPS = 1e-06
MESH = pl.DeviceIdType.MESH
F32 = jnp.float32
BF16 = jnp.bfloat16

NX, NZ, NC, NY = 4, 16, 2, 4
NDP = NX * NZ * NC
NPEER = NX * NC
HALF = NZ // 2
RUN = 4
CAP = 3
LANES = 128
XFIRST = 256
APARTS = 4
EPARTS = 4
KINDS = 8


def coords():
    dp = lax.axis_index("dp")
    y = lax.axis_index("mp")
    core = lax.rem(dp, NC)
    chip = lax.div(dp, NC)
    return lax.div(chip, NZ), y, lax.rem(chip, NZ), core


def dp_index(x, z, core):
    return (x * NZ + z) * NC + core


def wrap(value, size):
    return lax.rem(value + 2 * size, size)


def remote(src, dst, send_sem, recv_sem, dp, y):
    return pltpu.make_async_remote_copy(
        src_ref=src,
        dst_ref=dst,
        send_sem=send_sem,
        recv_sem=recv_sem,
        device_id=(dp, y),
        device_id_type=MESH,
    )


def nt(a, b):
    return lax.dot_general(a, b, (((1,), (1,)), ((), ())), preferred_element_type=F32)


def mm(a, b):
    return jnp.dot(a, b, preferred_element_type=F32)


def onehot(mask):
    return jnp.where(mask, 1.0, 0.0).astype(BF16)


def iota(shape, dim):
    return lax.broadcasted_iota(jnp.int32, shape, dim)


def down(mask, value):
    return jnp.sum(jnp.where(mask, value, 0.0), axis=0, keepdims=True)


def across(mask, value):
    return jnp.sum(jnp.where(mask, value, 0.0), axis=1, keepdims=True)


def greet(peers):
    barrier = pltpu.get_barrier_semaphore()
    for dp, y in peers:
        pl.semaphore_signal(barrier, inc=1, device_id=(dp, y), device_id_type=MESH)
    pl.semaphore_wait(barrier, len(peers))


def run_table(neg_ref, rows):
    holder = iota((rows, LANES), 1)
    query = iota((rows, LANES), 0).astype(F32)
    holder = dp_index(
        lax.div(holder, NZ * NC), lax.rem(holder, NZ), lax.rem(lax.div(holder, NZ), NC)
    ).astype(F32)
    before = onehot(iota((rows, rows), 1) < iota((rows, rows), 0))
    base = jnp.zeros((1, LANES), F32)
    passages = [base] * RUN
    queries = [base] * CAP
    ids = neg_ref[...]
    turn = onehot(iota((rows, rows), 0) == iota((rows, rows), 1))
    owners = nt(turn, lax.div(ids, rows).astype(F32).astype(BF16))
    locals_ = nt(turn, lax.rem(ids, rows).astype(F32).astype(BF16))
    for r in range(neg_ref.shape[0] // RUN):
        hit = owners[:, RUN * r : RUN * r + 1] == holder
        rank = mm(before, onehot(hit)) + base
        base = base + jnp.sum(jnp.where(hit, 1.0, 0.0), axis=0, keepdims=True)
        for i in range(CAP):
            queries[i] = queries[i] + down(hit & (rank == float(i)), query + 1.0)
        for j in range(RUN):
            local = locals_[:, RUN * r + j : RUN * r + j + 1]
            named = jnp.max(jnp.where(hit, local, 0.0), axis=0, keepdims=True)
            passages[j] = jnp.maximum(passages[j], named)
    return jnp.concatenate(passages + [q - 1.0 for q in queries] + [jnp.full((1, LANES), -1.0)], 0)


def seen_z(z, step, second):
    ahead = jnp.where(step == 0, HALF, step)
    return lax.rem(jnp.where(second == 0, z - step + NZ, z + ahead), NZ)


def fill_picks(tab, sel_ref, rank, z, rows):
    lane8 = iota((NPEER, LANES), 1)
    row8 = iota((NPEER, LANES), 0)
    row = iota((LANES, LANES), 0)
    lane = iota((LANES, LANES), 1)
    kind = lax.rem(lane8, KINDS)
    second = lax.rem(lax.div(lane8, KINDS), 2)
    kind_l = lax.rem(lane, KINDS)
    second_l = lax.rem(lax.div(lane, KINDS), 2)
    group_l = lax.div(lane, 2 * KINDS)
    asked = jnp.concatenate([tab[d, z] for d in range(NPEER) for _ in range(2)], axis=0).astype(BF16)
    zero8 = jnp.zeros_like(row8)
    firsts = nt(onehot(lane8 == rank * NZ + seen_z(z, row8, zero8)), asked)
    seconds = nt(onehot(lane8 == rank * NZ + seen_z(z, row8, zero8 + 1)), asked)
    from_p = jnp.where(second == 0, firsts, seconds) + float(rows)
    here = tab[rank].reshape(LANES, LANES).astype(BF16)
    spread = mm(here, onehot(row == group_l * NZ + z))
    from_q = jnp.concatenate(
        [
            down(row == seen_z(z, jnp.full_like(lane, s), second_l) * KINDS + kind_l, spread)
            for s in range(HALF)
        ],
        axis=0,
    )
    picked = jnp.where(kind < RUN, from_p, from_q)
    picked = jnp.where(picked >= 0.0, picked + (second * 2 * rows).astype(F32), -1.0)
    sel_ref[...] = picked.astype(jnp.int32)


def about_this(tab, rank, z):
    lane8 = iota((NPEER, LANES), 1)
    row = iota((LANES, LANES), 0)
    lane = iota((LANES, LANES), 1)
    me_row = onehot(lane8 == rank * NZ + z)
    said = [nt(me_row, tab[d].reshape(LANES, LANES).astype(BF16))[0:1] for d in range(NPEER)]
    said = jnp.concatenate(said, axis=0)
    low = said.astype(BF16)
    first = lane - lax.rem(lane, KINDS)
    passages = [mm(low, onehot(row == first + r)) for r in range(RUN)]
    return jnp.concatenate([said] + passages, axis=0).astype(BF16)


def fill_meets(tab, about, idx_ref, step, rank, z, rows):
    row = iota((LANES, LANES), 0)
    lane = iota((LANES, LANES), 1)
    kind_l = lax.rem(lane, KINDS)
    group_l = lax.div(lane, 2 * KINDS)
    z_l = seen_z(z, jnp.full_like(lane, step), lax.rem(lax.div(lane, KINDS), 2))
    kind = kind_l[0:1]
    own = mm(tab[rank, z].astype(BF16), onehot(row == group_l * NZ + z_l))
    found = mm(about, onehot(row == z_l * KINDS + kind_l))
    from_peer = row[0:NPEER] == group_l[0:NPEER]
    picked = [down(from_peer, found[NPEER * k : NPEER * (k + 1)]) for k in range(RUN + 1)]
    wants = picked[0]
    out = []
    for r in range(RUN):
        theirs = jnp.where(wants >= 0.0, picked[1 + r] + float(rows), -1.0)
        out.append(jnp.where(kind < RUN, own[RUN + r : RUN + r + 1], theirs))
    out.append(jnp.where(kind < RUN, -1.0, wants))
    out += [jnp.full((1, LANES), -1.0)] * (8 - len(out))
    idx_ref[step] = jnp.concatenate(out, axis=0).astype(jnp.int32)


def fused_kernel(
    hq_ref,
    hp_ref,
    w_ref,
    neg_ref,
    pos_ref,
    gq_ref,
    gp_ref,
    loss_ref,
    hid,
    wbuf,
    tab,
    sel_ref,
    idx_ref,
    col,
    outbox,
    recv,
    ybuf,
    dz,
    dtab,
    gpart,
    gin,
    acc,
    h_s,
    h_r,
    t_s,
    t_r,
    u_s,
    u_r,
    a_s,
    a_r,
    b_s,
    b_r,
    ax_s,
    ax_r,
    bx_s,
    bx_r,
    bd_s,
    bd_r,
    c_s,
    c_r,
    z_s,
    z_r,
    p_s,
    p_r,
    y_s,
    y_r,
    d_s,
    d_r,
    e_s,
    e_r,
    g_s,
    g_r,
):
    x, y, z, core = coords()
    me = dp_index(x, z, core)
    rank = x * NC + core
    rows, width = hq_ref.shape
    rows2 = 2 * rows
    depth = w_ref.shape[0]
    right = dp_index(x, wrap(z + 1, NZ), core)
    left = dp_index(x, wrap(z - 1, NZ), core)
    x_next = dp_index(wrap(x + 1, NX), z, core)
    x_prev = dp_index(wrap(x - 1, NX), z, core)
    sibling = dp_index(x, z, 1 - core)

    def peer_of(k):
        other = wrap(rank + k, NPEER)
        return dp_index(lax.div(other, NC), z, lax.rem(other, NC))

    y_peers = [wrap(y + k, NY) for k in range(1, NY)]
    z_peers = [dp_index(x, wrap(z + k, NZ), core) for k in range(1, NZ)]
    mates = [peer_of(k) for k in range(1, NPEER)]
    greet([(me, p) for p in y_peers] + [(right, y), (left, y)] + [(p, y) for p in mates])

    def send(src, dst, send_sem, recv_sem, dp, at_y):
        cp = remote(src, dst, send_sem, recv_sem, dp, at_y)
        cp.start()
        return cp

    def drain(ref, sem):
        pltpu.make_async_copy(ref, ref, sem).wait()

    def base_of(zb):
        return pl.multiple_of((zb * NC + core) * depth, depth)

    first_cols = pl.ds(0, XFIRST)
    other_cols = pl.ds(XFIRST, width - XFIRST)

    def a_block(zb, lo, count):
        return wbuf.at[pl.ds(lo, count), pl.ds(base_of(zb), depth), first_cols]

    def b_block(xb, zb, lo=0, count=depth):
        return wbuf.at[xb, pl.ds(pl.multiple_of(base_of(zb) + lo, count), count), other_cols]

    def z_of(block):
        if block <= HALF:
            return wrap(z - block, NZ)
        return wrap(z + block - HALF, NZ)

    def a_ring(direction, step, piece):
        zb = wrap(z - (step - 1), NZ) if direction == 0 else wrap(z + (step - 1), NZ)
        part = a_block(zb, piece * (NX // APARTS), NX // APARTS)
        to = right if direction == 0 else left
        at = (direction, step - 1, piece)
        return send(part, part, a_s, a_r.at[at], to, y)

    def t_ring(direction, step):
        zb = wrap(z - (step - 1), NZ) if direction == 0 else wrap(z + (step - 1), NZ)
        part = tab.at[rank, zb]
        to = right if direction == 0 else left
        return send(part, part, t_s, t_r.at[direction, step - 1], to, y)

    def b_ring(direction, step):
        zb = wrap(z - (step - 1), NZ) if direction == 0 else wrap(z + (step - 1), NZ)
        if step < HALF:
            part = b_block(x, zb)
        else:
            part = b_block(x, zb, direction * (depth // 2), depth // 2)
        to = right if direction == 0 else left
        return send(part, part, b_s, b_r.at[direction, step - 1], to, y)

    def b_over_x(block):
        part = b_block(x, z_of(block))
        return [
            send(part, part, bx_s, bx_r.at[way, block], to, y)
            for way, to in ((0, x_next), (1, x_prev))
        ]

    def b_across(block, copies):
        for way, to in ((0, x_next), (1, x_prev)):
            copies[way].wait_recv()
            xb = wrap(x - 1, NX) if way == 0 else wrap(x + 1, NX)
            part = b_block(xb, z_of(block), way * (depth // 2), depth // 2)
            send(part, part, bd_s, bd_r.at[block], to, y)

    def to_sibling(cols, block):
        part = wbuf.at[:, pl.ds(base_of(z_of(block)), depth), cols]
        send(part, part, c_s, c_r, sibling, y)

    wbuf[x, pl.ds(base_of(z), depth), :] = w_ref[...]
    own_first = wbuf.at[x, pl.ds(base_of(z), depth), first_cols]
    for k in range(1, NX):
        send(own_first, own_first, ax_s, ax_r, dp_index(wrap(x + k, NX), z, core), y)
    b_live = {(way, 1): b_ring(way, 1) for way in range(2)}
    over_x = {0: b_over_x(0)}
    hid[y, 0:rows, :] = hq_ref[...]
    hid[y, rows:rows2, :] = hp_ref[...]
    for peer in y_peers:
        send(hid.at[y], hid.at[y], h_s, h_r, me, peer)
    drain(wbuf.at[0, pl.ds(0, (NX - 1) * depth), first_cols], ax_r)
    a_live = {}
    for piece in range(APARTS):
        for way in range(2):
            a_live[way, 1, piece] = a_ring(way, 1, piece)
    to_sibling(first_cols, 0)

    tab[rank, z] = run_table(neg_ref, rows)
    t_live = {(way, 1): t_ring(way, 1) for way in range(2)}

    blocks_of = {0: [0]}
    for step in range(1, HALF):
        blocks_of[step] = [step, HALF + step]
    blocks_of[HALF] = [HALF]

    def finish(step):
        for block in blocks_of[step]:
            drain(b_block(x, z), bd_r.at[block])
            to_sibling(other_cols, block)

    def turn(step):
        for block in blocks_of[step]:
            b_across(block, over_x[block])

    for turn_at in range(1, HALF + 2):
        step = turn_at
        if step <= HALF:
            for way in range(2):
                b_live[way, step].wait_recv()
                if step < HALF:
                    b_live[way, step + 1] = b_ring(way, step + 1)
                    over_x[blocks_of[step][way]] = b_over_x(blocks_of[step][way])
            if step == HALF:
                over_x[HALF] = b_over_x(HALF)
        step = turn_at - 1
        if step >= 1:
            for piece in range(APARTS):
                for way in range(2):
                    if (way, step, piece) not in a_live:
                        continue
                    a_live[way, step, piece].wait_recv()
                    if step + 1 < HALF or (step + 1 == HALF and piece * 2 // APARTS == way):
                        a_live[way, step + 1, piece] = a_ring(way, step + 1, piece)
            for way in range(2):
                if (way, step) in t_live:
                    t_live[way, step].wait_recv()
                    if step + 1 < HALF or (step + 1 == HALF and way == 0):
                        t_live[way, step + 1] = t_ring(way, step + 1)
            for block in blocks_of[step]:
                to_sibling(first_cols, block)
        turn(turn_at - 1)
        if turn_at >= 3:
            finish(turn_at - 3)
    for k, peer in enumerate(mates):
        send(tab.at[rank], tab.at[rank], u_s, u_r, peer, y)
    for step in range(HALF - 1, HALF + 1):
        finish(step)
    drain(wbuf.at[:, pl.ds(0, NZ * depth)], c_r)
    drain(hid.at[pl.ds(0, NY - 1)], h_r)

    tile = width // EPARTS

    def ring(direction, step, piece):
        src_at = 0 if direction == 0 or step == 1 else rows2
        cols = pl.ds(piece * tile, tile)
        src = col.at[step - 1, pl.ds(src_at, rows2), cols]
        if step < HALF:
            dst = col.at[step, pl.ds(direction * rows2, rows2), cols]
        else:
            dst = col.at[0, pl.ds(rows2, rows2), cols]
        to = right if direction == 0 else left
        at = (direction, step - 1, piece)
        return send(src, dst, z_s, z_r.at[at], to, y)

    live = {}
    for piece in range(EPARTS):
        total = jnp.zeros((rows2, tile), F32)
        for b in range(NY):
            total = total + mm(hid[b], wbuf[b, :, piece * tile : (piece + 1) * tile])
        col[0, 0:rows2, piece * tile : (piece + 1) * tile] = total.astype(BF16)
        for direction in range(2):
            live[direction, 1, piece] = ring(direction, 1, piece)
    drain(tab.at[pl.ds(0, NPEER - 1)], u_r)
    fill_picks(tab, sel_ref, rank, z, rows)
    about = about_this(tab, rank, z)

    lane = iota((1, rows2), 1)
    row_id = iota((rows2, rows2), 0)
    lane_id = iota((rows2, rows2), 1)
    eye = row_id == lane_id
    emb = col[0, 0:rows2, :]
    local = lax.rem(pos_ref[...], rows)
    partner = jnp.concatenate([local, local], axis=1).astype(F32)
    partner_col = across(eye, partner).astype(jnp.int32)
    partner = partner.astype(jnp.int32)
    pair = ((lane_id < rows) & (row_id == partner + rows)) | (
        (row_id < rows) & (lane_id == partner_col + rows)
    )
    gram = nt(emb, emb)
    own_sq = down(eye, gram)
    own_pos = down(pair, gram)

    def mask_of(s, r):
        return row_id == idx_ref[s, r : r + 1, :]

    def score(s):
        fill_meets(tab, about, idx_ref, s, rank, z, rows)
        drain(recv.at[s, pl.ds(0, NPEER - 1)], p_r.at[s])
        got = recv[s].reshape(rows2, width)
        cross = nt(emb, got)
        parts = [down(mask_of(s, r), cross) for r in range(RUN)]
        parts += [down(eye, nt(got, got)), own_sq, own_pos, jnp.zeros_like(own_sq)]
        ybuf[y, s] = jnp.concatenate(parts, axis=0)

    pair_rows = iota((2 * rows2, LANES), 0)
    for step in range(1, HALF + 1):
        for piece in range(EPARTS):
            for direction in range(2):
                if (direction, step, piece) not in live:
                    continue
                live[direction, step, piece].wait_recv()
                if step + 1 < HALF or (step + 1 == HALF and piece * 2 // EPARTS == direction):
                    live[direction, step + 1, piece] = ring(direction, step + 1, piece)
        slot = step % HALF
        pick = onehot(pair_rows == sel_ref[slot : slot + 1, :])
        picked = lax.dot_general(
            pick, col[slot], (((0,), (0,)), ((), ())), preferred_element_type=F32
        )
        outbox[slot] = picked.astype(BF16).reshape(NPEER, 2 * KINDS, width)
        for k, peer in enumerate(mates):
            src = outbox.at[slot, wrap(rank + k + 1, NPEER)]
            send(src, recv.at[slot, rank], p_s, p_r.at[slot], peer, y)
        recv[slot, rank] = outbox[slot, rank]
        if step > 1:
            score(step - 1)
    most = ybuf.at[y, pl.ds(1, HALF - 1)]
    for peer in y_peers:
        send(most, most, y_s, y_r, me, peer)
    score(0)

    for peer in y_peers:
        send(ybuf.at[y, 0], ybuf.at[y, 0], y_s, y_r, me, peer)
    drain(ybuf.at[pl.ds(0, NY - 1)], y_r)

    sums = [((ybuf[0, s] + ybuf[1, s]) + ybuf[2, s]) + ybuf[3, s] for s in range(HALF)]
    inv_row = 1.0 / jnp.sqrt(sums[0][5:6] + EPS)
    inv_col = across(eye, inv_row)
    pos_score = SCALE * sums[0][6:7] * inv_row * down(pair, inv_col)
    pos_exp = jnp.exp(pos_score)
    denom = across(eye, pos_exp)
    scores = []
    exps = []
    lane_inv = []
    for d in range(HALF):
        rl = 1.0 / jnp.sqrt(sums[d][4:5] + EPS)
        lane_inv.append(rl)
        sc = []
        ex = []
        for r in range(RUN):
            mask = mask_of(d, r)
            s = SCALE * sums[d][r : r + 1] * rl * down(mask, inv_col)
            e = jnp.exp(s)
            sc.append(s)
            ex.append(e)
            denom = denom + across(mask, e)
        scores.append(sc)
        exps.append(ex)
    denom_row = down(eye, denom)
    loss_ref[...] = jnp.log(denom_row[:, 0:rows]) - pos_score[:, 0:rows]
    is_query = lane < rows
    dinv_row = jnp.where(is_query, 1.0 / denom_row, 0.0)
    dinv_col = across(eye, dinv_row)

    dz[0] = dinv_row
    for k, peer in enumerate(z_peers):
        send(dz.at[0], dz.at[k + 1], d_s, d_r, peer, y)

    pos_coef = jnp.where(is_query, SCALE * (pos_exp * dinv_row - 1.0), 0.0)
    pos_coef = pos_coef + down(pair, across(eye, pos_coef))

    def half(part):
        return slice(part * rows, (part + 1) * rows)

    def half_weights(part, dinv_at):
        half_id = iota((rows, rows2), 0) + part * rows
        weights = []
        inners = []
        for s in range(HALF):
            weight = jnp.zeros((rows, rows2), F32)
            inner = jnp.zeros((rows, rows2), F32)
            for r in range(RUN):
                mask = half_id == idx_ref[s, r : r + 1, :]
                coef = exps[s][r] * dinv_at(s, r)
                weight = weight + jnp.where(mask, SCALE * coef * lane_inv[s], 0.0)
                inner = inner + jnp.where(mask, coef * scores[s][r], 0.0)
            weights.append(weight)
            inners.append(inner)
        return weights, inners

    def half_grads(part, weights, inner):
        def weighted(weight, values):
            high = weight.astype(BF16)
            low = (weight - high.astype(F32)).astype(BF16)
            term = mm(jnp.concatenate([high, low], axis=0), values)
            return term[0:rows] + term[rows:]

        half_pair = pair[half(part)]
        inner = jnp.sum(inner, axis=1, keepdims=True)
        inner = inner + across(half_pair, pos_coef * pos_score * (1.0 / SCALE))
        arrived = recv[...].reshape(HALF * rows2, width)
        acc[...] = weighted(jnp.where(half_pair, pos_coef * inv_row, 0.0), emb) + weighted(
            jnp.concatenate(weights, axis=1), arrived
        )
        unit = emb[half(part)].astype(F32) * inv_col[half(part)]
        return ((acc[...] - unit * inner) * inv_col[half(part)]).astype(BF16)

    def project(part, g_emb):
        for k in (2, 1, 3, NY):
            block = wrap(y + k, NY)
            gpart[part, k - 1] = nt(g_emb, wbuf[block]).astype(BF16)
            if k < NY:
                mine = gpart.at[part, k - 1]
                theirs = gin.at[part, k - 1]
                send(mine, theirs, g_s, g_r.at[part], me, block)

    def gathered(part):
        total = gpart[part, NY - 1].astype(F32)
        drain(gin.at[part], g_r.at[part])
        for k in range(NY - 1):
            total = total + gin[part, k].astype(F32)
        return total.astype(BF16)

    weights, inners = half_weights(0, lambda s, r: down(mask_of(s, r), dinv_col))
    g_query = half_grads(0, weights, sum(inners))
    drain(dz.at[pl.ds(0, NZ - 1)], d_r)
    for k, peer in enumerate(mates):
        send(dz, dtab.at[k + 1], e_s, e_r, peer, y)
    for k in range(NZ):
        dtab[0, k] = dz[k]
    project(0, g_query)

    weights, inners = half_weights(1, lambda s, r: 1.0)
    drain(dtab.at[pl.ds(0, NPEER - 1)], e_r)
    at_source = iota((NZ, rows2), 0) == lax.div(iota((NZ, rows2), 1), KINDS)
    inner = jnp.zeros((rows, rows2), F32)
    for s in range(HALF):
        ahead = (s, NZ - s) if s else (0, HALF)
        table = [dtab[wrap(rank - d, NPEER), k] for d in range(NPEER) for k in ahead]
        table = jnp.concatenate(table, axis=0)
        high = table.astype(BF16)
        rest = table - high.astype(F32)
        middle = rest.astype(BF16)
        low = (rest - middle.astype(F32)).astype(BF16)
        spread = onehot(row_id == idx_ref[s, RUN : RUN + 1, :])
        found = mm(jnp.concatenate([high, middle, low], axis=0), spread)
        found = (found[0:NZ] + found[NZ : 2 * NZ]) + found[2 * NZ :]
        their_inv = down(at_source, found)
        weights[s] = weights[s] * their_inv
        inner = inner + inners[s] * their_inv
    project(1, half_grads(1, weights, inner))
    gq_ref[...] = gathered(0)
    gp_ref[...] = gathered(1)

    drain(hid.at[pl.ds(0, NY - 1)], h_s)
    drain(tab.at[0, pl.ds(0, NZ - 1)], t_s)
    drain(tab.at[pl.ds(0, NPEER - 1)], u_s)
    drain(wbuf.at[:, pl.ds(0, (NZ - 1) * depth), first_cols], a_s)
    drain(wbuf.at[0, pl.ds(0, (NZ - 1) * depth), other_cols], b_s)
    drain(wbuf.at[0, pl.ds(0, (NX - 1) * depth), first_cols], ax_s)
    drain(wbuf.at[0, pl.ds(0, 2 * NZ * depth), other_cols], bx_s)
    drain(wbuf.at[0, pl.ds(0, NZ * depth), other_cols], bd_s)
    drain(wbuf.at[:, pl.ds(0, NZ * depth)], c_s)
    drain(col.at[:, pl.ds(0, rows2 * (NZ - 1) // HALF)], z_s)
    drain(outbox.at[:, pl.ds(0, NPEER - 1)], p_s)
    drain(ybuf.at[pl.ds(0, NY - 1)], y_s)
    drain(dz.at[pl.ds(0, NZ - 1)], d_s)
    drain(dtab.at[pl.ds(0, NPEER - 1)], e_s)
    drain(gin, g_s)


def body(q_hidden, p_hidden, proj, positives, negatives):
    rows, width = q_hidden.shape
    rows2 = 2 * rows
    block = proj.shape[0] * NDP // NX
    vmem = pl.BlockSpec(memory_space=pltpu.VMEM)
    dma = pltpu.SemaphoreType.DMA

    grad_q, grad_p, loss = pl.pallas_call(
        fused_kernel,
        out_shape=(
            jax.ShapeDtypeStruct((rows, width), BF16),
            jax.ShapeDtypeStruct((rows, width), BF16),
            jax.ShapeDtypeStruct((1, rows), F32),
        ),
        in_specs=[vmem] * 5,
        out_specs=(vmem,) * 3,
        scratch_shapes=[
            pltpu.VMEM((NY, rows2, width), BF16),
            pltpu.VMEM((NX, block, width), BF16),
            pltpu.VMEM((NPEER, NZ, 8, LANES), F32),
            pltpu.VMEM((HALF, LANES), jnp.int32),
            pltpu.VMEM((HALF, 8, LANES), jnp.int32),
            pltpu.VMEM((HALF, 2 * rows2, width), BF16),
            pltpu.VMEM((HALF, NPEER, 2 * KINDS, width), BF16),
            pltpu.VMEM((HALF, NPEER, 2 * KINDS, width), BF16),
            pltpu.VMEM((NY, NPEER, 8, rows2), F32),
            pltpu.VMEM((NZ, 1, rows2), F32),
            pltpu.VMEM((NPEER, NZ, 1, rows2), F32),
            pltpu.VMEM((2, NY, rows, width), BF16),
            pltpu.VMEM((2, NY - 1, rows, width), BF16),
            pltpu.VMEM((rows, width), F32),
        ]
        + [dma, dma]
        + [dma, dma((2, HALF))]
        + [dma, dma]
        + [dma, dma((2, HALF, APARTS))]
        + [dma, dma((2, HALF))]
        + [dma, dma]
        + [dma, dma((2, NZ))]
        + [dma, dma((NZ,))]
        + [dma, dma]
        + [dma, dma((2, HALF, EPARTS))]
        + [dma, dma((HALF,))]
        + [dma, dma]
        + [dma, dma]
        + [dma, dma]
        + [dma, dma((2,))],
        compiler_params=pltpu.CompilerParams(
            collective_id=0, has_side_effects=True, vmem_limit_bytes=56 * 1024 * 1024
        ),
        cost_estimate=pl.CostEstimate(
            flops=3 * 10**9, bytes_accessed=10**8, transcendentals=10**5
        ),
        name="contrastive_backward",
    )(q_hidden, p_hidden, proj, negatives.T, positives[None, :])
    return (grad_q, grad_p, loss[0])


def solution(mesh):
    placed = (P("dp", "mp"), P("dp", "mp"), P("dp", "mp"), P("dp"), P("dp", None))
    return jax.shard_map(
        body,
        mesh=mesh,
        in_specs=placed,
        out_specs=(P("dp", "mp"), P("dp", "mp"), P("dp")),
        check_vma=False,
    )
```
